256 devices in a mesh: row: 16 (over x, y_lo, core), col: 16 (over z, y_hi).
Axes of the slice: x: 4, y: 4 (y_hi: 2, y_lo: 2; y = y_hi * 2 + y_lo), z: 8, core: 2. Of those that a mesh axis runs over, the one named last changes fastest.
Arguments:
- tokens: float32 [2048, 2048, 128], P('row', 'col'), may hold values from -6 to 6
- regions: int32 [2048, 2048], P('row', 'col'), may hold values from 0 to 15, as said below
- rel_index: int32 [64, 64], replicated, may hold values from 0 to 224, as said below
- bias_table: float32 [225, 4], replicated, may hold values from -215 to 215
- norm1_gain: float32 [128], replicated, may hold values from 0.1 to 1.9
- w_qkv: bfloat16 [128, 384], replicated, may hold values from -0.5 to 0.5
- w_proj: bfloat16 [128, 128], replicated, may hold values from -0.5 to 0.5
- norm2_gain: float32 [128], replicated, may hold values from 0.1 to 1.9
- w_up: bfloat16 [128, 512], replicated, may hold values from -0.5 to 0.5
- w_down: bfloat16 [512, 128], replicated, may hold values from -0.25 to 0.25
- merge_gain: float32 [512], replicated, may hold values from 0.1 to 1.9
- w_merge: bfloat16 [512, 256], replicated, may hold values from -0.25 to 0.25
Outputs:
- merged: bfloat16 [1024, 1024, 256], P('row', 'col')
The draws below stay inside these ranges and needn't reach their ends.
Inputs may be any that keep to these rules, and one draw needn't show every extreme that they name: `regions`: constant on strips of 16 token rows and 16 token columns. `rel_index`: entries of one value belong to a single relative offset; every entry of the table is used.
All inputs are finite; a program needn't handle non-finite values.
Results may differ from the reference program's by a relative error of at most 0.011.
Values may be sent and summed in bfloat16 or wider, within the bound.
No kernel may reach another device: no remote copies, remote signals or barrier semaphores. Data moves between devices by JAX's collectives and lax.ppermute only.
A program may use at most 128 MiB of HBM per device.

```python
import jax
import jax.numpy as jnp
from jax import lax

C = 128
HEADS = 4
HD = 32
MLP = 512
WIN = 8
SHIFT = 4
TABLE = 225
H = 2048
W = 2048


def draw_regions(key, part):
    key = jax.random.fold_in(key, 11)
    key_rows, key_cols = jax.random.split(key)
    strips_r = H // 16
    strips_c = W // 16
    row_labels = jax.random.permutation(key_rows, jnp.arange(strips_r, dtype=jnp.int32) % 4)
    col_labels = jax.random.permutation(key_cols, jnp.arange(strips_c, dtype=jnp.int32) % 4)
    row_full = jnp.repeat(row_labels, 16)
    col_full = jnp.repeat(col_labels, 16)
    return (row_full[:, None] * 4 + col_full[None, :]).astype(jnp.int32)


def draw_rel_index(key, part):
    key = jax.random.fold_in(key, 23)
    order = jax.random.permutation(key, jnp.arange(TABLE, dtype=jnp.int32))
    spots = jnp.arange(WIN * WIN, dtype=jnp.int32)
    along_y = spots // WIN
    along_x = spots % WIN
    delta_y = along_y[:, None] - along_y[None, :] + WIN - 1
    delta_x = along_x[:, None] - along_x[None, :] + WIN - 1
    base = delta_y * (2 * WIN - 1) + delta_x
    return order[base].astype(jnp.int32)


def draw_bias_table(key, part):
    key = jax.random.fold_in(key, 37)
    table = jax.random.normal(key, (TABLE, HEADS), jnp.float32)
    return table


def shard_levels(own_key, shape, cuts, smallest, high):
    def one(axis_at, blocks):
        heights = jax.random.uniform(jax.random.fold_in(jax.random.fold_in(own_key, 6), axis_at), (blocks,), jnp.float32, smallest / len(cuts), high / len(cuts))
        return jnp.repeat(jnp.exp(heights), shape[axis_at] // blocks).reshape((-1,) + (1,) * (len(shape) - axis_at - 1))

    factor_of = one(*cuts[0])
    for cut in cuts[1:]:
        factor_of = factor_of * one(*cut)
    return factor_of


def normal_values(stream_key, dims, spread, bound, cuts=(), held_as=jnp.bfloat16):
    values = spread * jax.random.normal(stream_key, dims, jnp.float32)
    if cuts:
        values = values * shard_levels(stream_key, dims, cuts, -0.22, 0.18)
    return jnp.clip(values, -bound, bound).astype(held_as)


def setup_inputs(seed: int = 0) -> dict:
    keys = jax.random.split(jax.random.key(seed), 13)
    return {
        "tokens": normal_values(keys[0], (H, W, C), 1.0, 6.0, ((0, 16), (1, 16)), jnp.float32),
        "regions": draw_regions(jax.random.fold_in(keys[12], 71), 0),
        "rel_index": draw_rel_index(jax.random.fold_in(keys[12], 71), 0),
        "bias_table": draw_bias_table(jax.random.fold_in(keys[12], 71), 0),
        "norm1_gain": jnp.clip(1.0 + 0.18 * jax.random.normal(keys[4], (C,), jnp.float32), 0.1, 1.9),
        "w_qkv": normal_values(keys[5], (C, 3 * C), C ** -0.5, 0.5),
        "w_proj": normal_values(keys[6], (C, C), C ** -0.5, 0.5),
        "norm2_gain": jnp.clip(1.0 + 0.18 * jax.random.normal(keys[7], (C,), jnp.float32), 0.1, 1.9),
        "w_up": normal_values(keys[8], (C, MLP), C ** -0.5, 0.5),
        "w_down": normal_values(keys[9], (MLP, C), MLP ** -0.5, 0.25),
        "merge_gain": jnp.clip(1.0 + 0.18 * jax.random.normal(keys[10], (4 * C,), jnp.float32), 0.1, 1.9),
        "w_merge": normal_values(keys[11], (4 * C, 2 * C), (4 * C) ** -0.5, 0.25),
    }


def layer_norm(values, gain):
    mean = lax.optimization_barrier(jnp.mean(values, axis=-1, keepdims=True))
    centred = values - mean
    var = lax.optimization_barrier(jnp.mean(centred * centred, axis=-1, keepdims=True))
    return centred / jnp.sqrt(var + 1e-05) * gain

def build_bias(rel_index, bias_table):
    onehot = (rel_index[:, :, None] == jnp.arange(TABLE, dtype=jnp.int32)[None, None, :]).astype(jnp.float32)
    return jnp.einsum('ijt,th->hij', onehot, bias_table, precision=lax.Precision.HIGHEST)

def window_row(rows_in, row_ids, bias, norm1_gain, w_qkv, w_proj, norm2_gain, w_up, w_down):
    width = rows_in.shape[1]
    count = width // WIN
    normed = layer_norm(rows_in, norm1_gain).astype(jnp.bfloat16)
    flat = normed.reshape(WIN, count, WIN, C).transpose(1, 0, 2, 3).reshape(count * WIN * WIN, C)
    labels = row_ids.reshape(WIN, count, WIN).transpose(1, 0, 2).reshape(count, WIN * WIN)
    qkv = jnp.dot(flat, w_qkv, preferred_element_type=jnp.float32).astype(jnp.bfloat16)
    qkv = qkv.reshape(count, WIN * WIN, 3, HEADS, HD).astype(jnp.float32)
    query, key, value = (qkv[:, :, 0], qkv[:, :, 1], qkv[:, :, 2])
    scores = jnp.einsum('wqhd,wkhd->whqk', query, key) * HD ** (-0.5) + bias[None]
    same = labels[:, :, None] == labels[:, None, :]
    scores = jnp.where(same[:, None], scores, -1e+30)
    top = lax.optimization_barrier(jnp.max(scores, axis=-1, keepdims=True))
    expo = jnp.exp(scores - top)
    probs = (expo / lax.optimization_barrier(jnp.sum(expo, axis=-1, keepdims=True))).astype(jnp.bfloat16)
    attended = jnp.einsum('whqk,wkhd->wqhd', probs.astype(jnp.float32), value).astype(jnp.bfloat16)
    attended = attended.reshape(count * WIN * WIN, C)
    projected = jnp.dot(attended, w_proj, preferred_element_type=jnp.float32)
    projected = projected.reshape(count, WIN, WIN, C).transpose(1, 0, 2, 3).reshape(WIN, width, C)
    middle = rows_in + projected
    second = layer_norm(middle, norm2_gain).astype(jnp.bfloat16).reshape(WIN * width, C)
    widened = jax.nn.gelu(jnp.dot(second, w_up, preferred_element_type=jnp.float32)).astype(jnp.bfloat16)
    down = jnp.dot(widened, w_down, preferred_element_type=jnp.float32)
    return middle + down.reshape(WIN, width, C)

def merge_patches(block, merge_gain, w_merge):
    joined = jnp.concatenate([block[0::2, 0::2], block[1::2, 0::2], block[0::2, 1::2], block[1::2, 1::2]], axis=-1)
    normed = layer_norm(joined, merge_gain).astype(jnp.bfloat16)
    rows_out, cols_out = (normed.shape[0], normed.shape[1])
    out = jnp.dot(normed.reshape(rows_out * cols_out, 4 * C), w_merge, preferred_element_type=jnp.float32)
    return out.astype(jnp.bfloat16).reshape(rows_out, cols_out, 2 * C)

def reference(tokens, regions, rel_index, bias_table, norm1_gain, w_qkv, w_proj, norm2_gain, w_up, w_down, merge_gain, w_merge):
    bias = build_bias(rel_index, bias_table)
    height = tokens.shape[0]

    def one_row(index):
        picks = (index * WIN + SHIFT + jnp.arange(WIN, dtype=jnp.int32)) % height
        picks = picks.astype(jnp.int32)
        rows_in = jnp.roll(jnp.take(tokens, picks, axis=0), -SHIFT, axis=1)
        row_ids = jnp.roll(jnp.take(regions, picks, axis=0), -SHIFT, axis=1)
        block = window_row(rows_in, row_ids, bias, norm1_gain, w_qkv, w_proj, norm2_gain, w_up, w_down)
        return merge_patches(block, merge_gain, w_merge)
    pieces = lax.map(one_row, jnp.arange(height // WIN, dtype=jnp.int32))
    merged = pieces.reshape(height // 2, tokens.shape[1] // 2, 2 * C)
    return jnp.roll(merged, (SHIFT // 2, SHIFT // 2), axis=(0, 1))
```

```python
import functools

import jax
import jax.numpy as jnp
from jax import lax
from jax.experimental import pallas as pl
from jax.experimental.pallas import tpu as pltpu
from jax.sharding import PartitionSpec as P

C = 128
HEADS = 4
HD = 32
WIN = 8
SPOTS = WIN * WIN
MLP = 512
SIDE = 128
OUT = SIDE // 2
STRIPS = SIDE // 16
IDROWS = 16
LOG2E = 1.4426950408889634
QSCALE = HD ** (-0.5) * LOG2E
VARIANTS = 24
F32 = jnp.float32
BF16 = jnp.bfloat16
NT = (((1,), (1,)), ((), ()))
TN = (((0,), (0,)), ((), ()))


def layer_norm(values, gain):
    mean = jnp.mean(values, axis=-1, keepdims=True)
    centred = values - mean
    var = jnp.mean(centred * centred, axis=-1, keepdims=True)
    return centred * lax.rsqrt(var + 1e-05) * gain


def half_gelu(half):
    h = half.astype(BF16)
    c0 = jnp.asarray(2.0 * 0.7978845608028654, BF16)
    c1 = jnp.asarray(8.0 * 0.7978845608028654 * 0.044715, BF16)
    inner = h * (c0 + c1 * (h * h))
    return h + h * jnp.tanh(inner)


def prepare(rel_ref, table_ref, w_qkv_ref, w_up_ref, bias_scr, wvt_scr, wup_scr, pad_scr):
    wvt_scr[...] = w_qkv_ref[:, 2 * C :].astype(F32).T.astype(BF16)
    wup_scr[...] = w_up_ref[...] * jnp.asarray(0.5, BF16)
    pad_scr[...] = jnp.zeros_like(pad_scr)
    pad_scr[pl.ds(0, table_ref.shape[0]), pl.ds(0, HEADS)] = table_ref[...]
    table_a = pad_scr[pl.ds(0, 128), :].T
    table_b = pad_scr[pl.ds(128, 128), :].T
    pad_scr[pl.ds(0, SPOTS), pl.ds(0, SPOTS)] = rel_ref[...].astype(F32)
    rel_t = pad_scr[pl.ds(0, 128), :].T[:SPOTS, :].astype(jnp.int32)
    rel_t = jnp.where(lax.broadcasted_iota(jnp.int32, (SPOTS, 128), 1) < SPOTS, rel_t, pltpu.roll(rel_t, SPOTS, 1))
    low = rel_t < 128
    spot = jnp.where(low, rel_t, rel_t - 128)
    lane = lax.broadcasted_iota(jnp.int32, (SPOTS, 128), 1)
    halves = []
    for pair in range(HEADS // 2):
        per_head = []
        for head in (2 * pair, 2 * pair + 1):
            row_a = jnp.broadcast_to(table_a[head : head + 1, :], (SPOTS, 128))
            row_b = jnp.broadcast_to(table_b[head : head + 1, :], (SPOTS, 128))
            got_a = jnp.take_along_axis(row_a, spot, axis=1, mode="promise_in_bounds")
            got_b = jnp.take_along_axis(row_b, spot, axis=1, mode="promise_in_bounds")
            per_head.append(jnp.where(low, got_a, got_b))
        halves.append(jnp.where(lane < SPOTS, per_head[0], per_head[1]) * LOG2E)
    bias = jnp.concatenate(halves, axis=1)
    key_spot = lax.broadcasted_iota(jnp.int32, (SPOTS, 2 * 128), 0)
    query_spot = lax.broadcasted_iota(jnp.int32, (SPOTS, 2 * 128), 1) % SPOTS

    def label_of(spots, labels):
        right = (spots % WIN) >= WIN // 2
        lower = spots >= SPOTS // 2
        top = jnp.where(right, labels[0], 0)
        low_row = jnp.where(right, labels[2], labels[1])
        return jnp.where(lower, low_row, top)

    def variant(index, carry):
        labels = (index // 12, (index // 4) % 3, index % 4)
        same = label_of(key_spot, labels) == label_of(query_spot, labels)
        bias_scr[index] = jnp.where(same, bias, -1e30)
        return carry

    lax.fori_loop(0, VARIANTS, variant, 0)


def pattern(top_left, top_right, low_left, low_right):
    one = jnp.where(top_right == top_left, 0, 1)
    two = jnp.where(low_left == top_left, 0, jnp.where(low_left == top_right, 1, 2))
    three = jnp.where(
        low_right == top_left,
        0,
        jnp.where(low_right == top_right, 1, jnp.where(low_right == low_left, 2, 3)),
    )
    return one * 12 + two * 4 + three


def front(loads, store_att, variants, w, bias_scr, wvt_scr):
    normed = []
    for load in loads:
        normed.append(layer_norm(load(), w["g1"][...]).astype(BF16))
        yield
    normed = jnp.concatenate(normed, axis=0)
    qk = jnp.dot(normed, w["w_qkv"][:, : 2 * C], preferred_element_type=F32)
    vt = lax.dot_general(wvt_scr[...], normed, NT, preferred_element_type=F32).astype(BF16)
    yield
    lane = lax.broadcasted_iota(jnp.int32, (1, C), 1)
    n = len(loads)
    st, ot = {}, {}
    for i in range(n + 2 * LAG):
        if i < n:
            rows = slice(SPOTS * i, SPOTS * (i + 1))
            q = (qk[rows, :C] * QSCALE).astype(BF16)
            k = qk[rows, C:].astype(BF16)
            qm = jnp.concatenate([jnp.where(lane // HD == h, q, jnp.zeros_like(q)) for h in range(HEADS)], axis=0)
            st[i] = lax.dot_general(k, qm, NT, preferred_element_type=F32)
        at = i - LAG
        if 0 <= at < n:
            rows = slice(SPOTS * at, SPOTS * (at + 1))
            scores = st.pop(at) + bias_scr[variants[at]]
            top = jnp.max(scores, axis=0, keepdims=True)
            p = jnp.exp2((scores - top).astype(BF16))
            vw = jnp.concatenate([vt[:, rows], jnp.ones((16, SPOTS), BF16)], axis=0)
            ot[at] = jnp.dot(vw, p, preferred_element_type=F32)
        at = i - 2 * LAG
        if 0 <= at < n:
            got = ot.pop(at)
            inv = 1.0 / got[C : C + 1]
            store_att(
                at,
                jnp.concatenate(
                    [
                        got[HD * h : HD * (h + 1), SPOTS * h : SPOTS * (h + 1)]
                        * inv[:, SPOTS * h : SPOTS * (h + 1)]
                        for h in range(HEADS)
                    ],
                    axis=0,
                ).astype(BF16),
            )
        yield


def back(loads, load_att, stores, w, wup_scr):
    proj = lax.dot_general(load_att(), w["w_proj"][...], TN, preferred_element_type=F32)
    yield
    mids, second = [], []
    for i, load in enumerate(loads):
        mids.append(load() + proj[SPOTS * i : SPOTS * (i + 1)])
        second.append(layer_norm(mids[-1], w["g2"][...]).astype(BF16))
        yield
    up = jnp.dot(jnp.concatenate(second, axis=0), wup_scr[...], preferred_element_type=F32)
    yield
    wide = []
    for i in range(len(loads)):
        wide.append(half_gelu(up[SPOTS * i : SPOTS * (i + 1)]))
        yield
    down = jnp.dot(jnp.concatenate(wide, axis=0), w["w_down"][...], preferred_element_type=F32)
    yield
    for i, store in enumerate(stores):
        store(mids[i] + down[SPOTS * i : SPOTS * (i + 1)])
        yield


LAG = 2


def merge(load_parts, store, w):
    joined = jnp.concatenate(load_parts(), axis=1)
    normed = layer_norm(joined, w["gm"][...]).astype(BF16)
    yield
    out = jnp.dot(normed, w["w_merge"][...], preferred_element_type=F32)
    yield
    store(out.astype(BF16))


def drive(timed):
    events = []
    for number, (start, gap, gen) in enumerate(timed):
        for step in range(80):
            events.append((start + gap * step, number, gen))
    for _, _, gen in sorted(events, key=lambda e: (e[0], e[1])):
        next(gen, None)


NAMES = ("g1", "w_qkv", "w_proj", "g2", "w_up", "w_down", "gm", "w_merge")
GROUP = 8
FRONT_EVERY, FRONT_GAP = 20, 1
BACK_EVERY, BACK_GAP = 16, 0.8
MERGE_EVERY, MERGE_GAP, MERGE_AT = 1.0, 1.0, 50


def interior_kernel(x_ref, old_ref, ids_ref, rel_ref, table_ref, *refs):
    w = dict(zip(NAMES, refs[:8]))
    out_ref, bias_scr, wvt_scr, wup_scr, pad_scr, att_scr, blk_scr = refs[8:]
    step = pl.program_id(0)
    count = SIDE // WIN - 1

    @pl.when(step == 0)
    def _():
        prepare(rel_ref, table_ref, w["w_qkv"], w["w_up"], bias_scr, wvt_scr, wup_scr, pad_scr)
        blk_scr[...] = jnp.zeros_like(blk_scr)

    upper, lower = step // 2, (step + 1) // 2

    def loader(ref, j):
        return lambda: jnp.concatenate([ref[y, pl.ds(WIN * j + 4, WIN), :] for y in range(WIN)], axis=0)

    def variant(j):
        left, right = 16 * (j // 2), 16 * ((j + 1) // 2)
        return pattern(ids_ref[upper, left], ids_ref[upper, right], ids_ref[lower, left], ids_ref[lower, right])

    def store_att(g):
        def store(i, value):
            att_scr[g, :, pl.ds(SPOTS * i, SPOTS)] = value

        return store

    def store_block(j):
        def store(value):
            for y in range(WIN):
                blk_scr[y, pl.ds(WIN * j + 4, WIN), :] = value[WIN * y : WIN * (y + 1)]

        return store

    groups = [list(range(at, min(at + GROUP, count))) for at in range(0, count, GROUP)]

    def fronts():
        return [
            (
                FRONT_EVERY * g,
                FRONT_GAP,
                front([loader(x_ref, j) for j in js], store_att(g), [variant(j) for j in js], w, bias_scr, wvt_scr),
            )
            for g, js in enumerate(groups)
        ]

    def backs():
        return [
            (
                BACK_EVERY * g,
                BACK_GAP,
                back(
                    [loader(old_ref, j) for j in js],
                    lambda g=g, js=js: att_scr[g, :, : SPOTS * len(js)],
                    [store_block(j) for j in js],
                    w,
                    wup_scr,
                ),
            )
            for g, js in enumerate(groups)
        ]

    def merges():
        def parts(a):
            return lambda: [blk_scr[2 * a + dy, pl.ds(dx, OUT, stride=2), :] for dx in range(2) for dy in range(2)]

        def store(a):
            def put(value):
                out_ref[a] = value

            return put

        return [(MERGE_AT + MERGE_EVERY * a, MERGE_GAP, merge(parts(a), store(a), w)) for a in range(4)]

    @pl.when(step == 0)
    def _():
        drive(fronts())

    @pl.when((step > 0) & (step < count))
    def _():
        drive(backs() + fronts() + merges())

    @pl.when(step == count)
    def _():
        drive(backs() + merges())


def whole(shape, space=pltpu.VMEM):
    return pl.BlockSpec(shape, lambda i: (0,) * len(shape), memory_space=space)


def interior(tokens, ids, rel_index, bias_table, weights):
    count = SIDE // WIN - 1
    last = count - 1
    return pl.pallas_call(
        interior_kernel,
        grid=(count + 1,),
        out_shape=jax.ShapeDtypeStruct((OUT, OUT, 2 * C), BF16),
        in_specs=[
            pl.BlockSpec(
                (pl.Element(WIN), pl.Element(SIDE), pl.Element(C)),
                lambda i: (WIN * jnp.minimum(i, last) + 4, 0, 0),
            ),
            pl.BlockSpec(
                (pl.Element(WIN), pl.Element(SIDE), pl.Element(C)),
                lambda i: (WIN * jnp.maximum(i - 1, 0) + 4, 0, 0),
            ),
            whole((STRIPS, SIDE), pltpu.SMEM),
            whole(rel_index.shape),
            whole(bias_table.shape),
        ]
        + [whole(a.shape) for a in weights],
        out_specs=pl.BlockSpec(
            (pl.Element(4), pl.Element(OUT), pl.Element(2 * C)), lambda i: (4 * jnp.maximum(i - 1, 0) + 2, 0, 0)
        ),
        scratch_shapes=[
            pltpu.VMEM((VARIANTS, SPOTS, HEADS * SPOTS), F32),
            pltpu.VMEM((C, C), BF16),
            pltpu.VMEM((C, MLP), BF16),
            pltpu.VMEM((256, 128), F32),
            pltpu.VMEM((pl.cdiv(count, GROUP), C, SPOTS * GROUP), BF16),
            pltpu.VMEM((WIN, SIDE, C), F32),
        ],
        compiler_params=pltpu.CompilerParams(vmem_limit_bytes=56 * 1024 * 1024),
    )(tokens, tokens, ids, rel_index, bias_table, *weights)


def edge_specs():
    return [
        pl.BlockSpec((4, SIDE, C), lambda i: (0, 0, 0)),
        pl.BlockSpec((4, SIDE, C), lambda i: (SIDE // 4 - 1, 0, 0)),
        pl.BlockSpec((SIDE, 8, C), lambda i: (0, 0, 0)),
        pl.BlockSpec((SIDE, 8, C), lambda i: (0, SIDE // 8 - 1, 0)),
    ]


def pack_kernel(top_ref, bottom_ref, left_ref, right_ref, regions_ref, ids_ref, *refs):
    messages, col_scr = refs[:8], refs[8]
    ids = regions_ref[pl.ds(0, STRIPS, stride=16), :]
    ids_ref[...] = ids
    coded = jnp.concatenate([ids, ids], axis=0).astype(F32).astype(BF16)
    line = 4 * SIDE
    for out, source in zip(messages[:2], (top_ref, bottom_ref)):
        for y in range(4):
            out[pl.ds(SIDE * y, SIDE), :] = source[y].astype(BF16)
    for out, source, at in zip(messages[2:4], (left_ref, right_ref), (0, 4)):
        for r in range(SIDE):
            col_scr[pl.ds(4 * r, 4), :] = source[r, pl.ds(at, 4), :]
        out[pl.ds(0, line), :] = col_scr[...].astype(BF16)
    for out in messages[:4]:
        out[pl.ds(line, IDROWS), :] = coded
    corners = ((top_ref, 0), (top_ref, SIDE - 4), (bottom_ref, 0), (bottom_ref, SIDE - 4))
    for out, (source, at) in zip(messages[4:], corners):
        for y in range(4):
            col_scr[pl.ds(4 * y, 4), :] = source[y, pl.ds(at, 4), :]
        out[pl.ds(0, 16), :] = col_scr[pl.ds(0, 16), :].astype(BF16)
        out[pl.ds(16, IDROWS), :] = coded


def pack(tokens, regions):
    line = jax.ShapeDtypeStruct((4 * SIDE + IDROWS, C), BF16)
    corner = jax.ShapeDtypeStruct((16 + IDROWS, C), BF16)
    shapes = [jax.ShapeDtypeStruct((STRIPS, SIDE), jnp.int32)] + [line] * 4 + [corner] * 4
    return pl.pallas_call(
        pack_kernel,
        grid=(1,),
        out_shape=shapes,
        in_specs=edge_specs() + [whole((SIDE, SIDE))],
        out_specs=[whole(a.shape) for a in shapes],
        scratch_shapes=[pltpu.VMEM((4 * SIDE, C), F32)],
    )(tokens, tokens, tokens, tokens, regions)


def exchange(messages):
    rows, cols = lax.axis_size("row"), lax.axis_size("col")

    def moved(value, down, along):
        if along == 0:
            return lax.ppermute(value, "row", [(i, (i + down) % rows) for i in range(rows)])
        if down == 0:
            return lax.ppermute(value, "col", [(i, (i + along) % cols) for i in range(cols)])
        pairs = [
            (r * cols + c, (r + down) % rows * cols + (c + along) % cols) for r in range(rows) for c in range(cols)
        ]
        return lax.ppermute(value, ("row", "col"), pairs)

    top, bottom, left, right, top_left, top_right, low_left, low_right = messages
    return (
        moved(bottom, 1, 0),
        moved(top, -1, 0),
        moved(right, 0, 1),
        moved(left, 0, -1),
        moved(low_right, 1, 1),
        moved(low_left, 1, -1),
        moved(top_right, -1, 1),
        moved(top_left, -1, -1),
    )


def gather_border(edges, got, x_scr, msg_scr):
    top, bottom, left, right = edges
    line = 4 * SIDE
    for n in range(4):
        msg_scr[pl.ds(line * n, line), :] = got[n][pl.ds(0, line), :].astype(F32)
    for n in range(4):
        msg_scr[pl.ds(4 * line + 16 * n, 16), :] = got[4 + n][pl.ds(0, 16), :].astype(F32)

    def row_of(n):
        return lambda y, at, size: msg_scr[pl.ds(line * n + SIDE * y + at, size), :]

    def col_of(n):
        return lambda r, at, size: msg_scr[pl.ds(line * n + 4 * r + at, size), :]

    def corner_of(n):
        return lambda y, at, size: msg_scr[pl.ds(4 * line + 16 * n + 4 * y + at, size), :]

    def own(ref):
        return lambda y, at, size: ref[y, pl.ds(at, size), :]

    above, below, from_left, from_right = row_of(0), row_of(1), col_of(2), col_of(3)
    for t in range(16):
        for y in range(8):
            spot = WIN * y
            side, at = (above, y) if y < 4 else (own(top), y - 4)
            if t == 0:
                edge = corner_of(0)(y, 0, 4) if y < 4 else from_left(y - 4, 0, 4)
                x_scr[0, t, pl.ds(spot, 4), :] = edge
                x_scr[0, t, pl.ds(spot + 4, 4), :] = side(at, 0, 4)
            else:
                x_scr[0, t, pl.ds(spot, 8), :] = side(at, 8 * t - 4, 8)
            side, at = (own(bottom), y) if y < 4 else (below, y - 4)
            if t == 15:
                edge = from_right(124 + y, 0, 4) if y < 4 else corner_of(3)(y - 4, 0, 4)
                x_scr[2, t, pl.ds(spot, 4), :] = side(at, 124, 4)
                x_scr[2, t, pl.ds(spot + 4, 4), :] = edge
            else:
                x_scr[2, t, pl.ds(spot, 8), :] = side(at, 8 * t + 4, 8)
            r = 8 * t - 4 + y
            x_scr[1, t, pl.ds(spot, 4), :] = above(y, 124, 4) if r < 0 else own(right)(r, 4, 4)
            x_scr[1, t, pl.ds(spot + 4, 4), :] = corner_of(1)(y, 0, 4) if r < 0 else from_right(r, 0, 4)
            r = 8 * t + 4 + y
            x_scr[3, t, pl.ds(spot, 4), :] = corner_of(2)(r - SIDE, 0, 4) if r >= SIDE else from_left(r, 0, 4)
            x_scr[3, t, pl.ds(spot + 4, 4), :] = below(r - SIDE, 0, 4) if r >= SIDE else own(left)(r, 0, 4)


def border_patterns(id_at, var_smem):
    for t in range(16):
        before = ((t + 1) // 2 - 1, t // 2)
        after = (t // 2, (t + 1) // 2)
        pairs = (((-1, 0), before), (before, (7, 8)), ((7, 8), after), (after, (-1, 0)))
        for s, (rs, cs) in enumerate(pairs):
            var_smem[s, t] = pattern(id_at(rs[0], cs[0]), id_at(rs[0], cs[1]), id_at(rs[1], cs[0]), id_at(rs[1], cs[1]))


def border_kernel(*refs):
    edges, own_ids, got = refs[:4], refs[4], refs[5:13]
    rel_ref, table_ref = refs[13:15]
    w = dict(zip(NAMES, refs[15:23]))
    inner_ref, out_ref = refs[23:25]
    (bias_scr, wvt_scr, wup_scr, pad_scr, att_scr, blk_scr, x_scr, msg_scr, idv_scr, ids_smem, var_smem, row_scr,
     col_scr, row_out, col_out, sem_ids, sem_in, sem_out) = refs[25:]
    step = pl.program_id(0)
    count = 16
    col_in = [
        pltpu.make_async_copy(inner_ref.at[:, pl.ds(at, 16), :], col_out.at[n], sem_in.at[n])
        for n, at in enumerate((0, OUT - 16))
    ]

    @pl.when(step == 0)
    def _():
        for copy in col_in:
            copy.start()
        for n in range(8):
            first = 4 * SIDE if n < 4 else 16
            idv_scr[pl.ds(STRIPS * n, STRIPS), :] = (
                got[n][pl.ds(first, IDROWS), :].astype(F32)[:STRIPS].astype(jnp.int32)
            )
        ids_copy = pltpu.make_async_copy(idv_scr, ids_smem, sem_ids)
        ids_copy.start()
        gather_border(edges, got, x_scr, msg_scr)
        prepare(rel_ref, table_ref, w["w_qkv"], w["w_up"], bias_scr, wvt_scr, wup_scr, pad_scr)
        ids_copy.wait()
        places = {(-1, 0): 0, (1, 0): 1, (0, -1): 2, (0, 1): 3, (-1, -1): 4, (-1, 1): 5, (1, -1): 6, (1, 1): 7}

        def id_at(m, n):
            where = (-1 if m < 0 else int(m >= STRIPS), -1 if n < 0 else int(n >= STRIPS))
            m, n = m % STRIPS, n % STRIPS
            if where == (0, 0):
                return own_ids[m, 16 * n]
            return ids_smem[STRIPS * places[where] + m, 16 * n]

        border_patterns(id_at, var_smem)

    groups = [list(range(at, at + GROUP)) for at in range(0, count, GROUP)]

    def store_att(g):
        def store(i, value):
            att_scr[g, :, pl.ds(SPOTS * i, SPOTS)] = value

        return store

    def store_block(t):
        def store(value):
            blk_scr[pl.ds(SPOTS * t, SPOTS), :] = value

        return store

    def fronts():
        return [
            (
                FRONT_EVERY * g,
                FRONT_GAP,
                front(
                    [lambda t=t: x_scr[step, t] for t in ts],
                    store_att(g),
                    [var_smem[step, t] for t in ts],
                    w,
                    bias_scr,
                    wvt_scr,
                ),
            )
            for g, ts in enumerate(groups)
        ]

    def backs():
        return [
            (
                BACK_EVERY * g,
                BACK_GAP,
                back(
                    [lambda t=t: x_scr[step - 1, t] for t in ts],
                    lambda g=g: att_scr[g],
                    [store_block(t) for t in ts],
                    w,
                    wup_scr,
                ),
            )
            for g, ts in enumerate(groups)
        ]

    @pl.when(step == 0)
    def _():
        drive(fronts())

    @pl.when((step > 0) & (step < 4))
    def _():
        drive(backs() + fronts())

    @pl.when(step == 4)
    def _():
        drive(backs())

    def spread(scr, at, first, value):
        for half in range(2):
            scr[2 * at + half, pl.ds(first, count, stride=4), :] = value[:, C * half : C * (half + 1)]

    def both(scr, at, rows):
        return jnp.concatenate([scr[2 * at + half, rows, :] for half in range(2)], axis=1)

    @pl.when(step > 0)
    def _():
        results = {}
        for a in range(4):
            joined = []
            for dx in range(2):
                for dy in range(2):
                    joined.append(
                        jnp.concatenate(
                            [
                                blk_scr[pl.ds((2 * a + dy) * WIN + 2 * b + dx, count, stride=SPOTS), :]
                                for b in range(4)
                            ],
                            axis=0,
                        )
                    )
            normed = layer_norm(jnp.concatenate(joined, axis=1), w["gm"][...]).astype(BF16)
            merged = jnp.dot(normed, w["w_merge"][...], preferred_element_type=F32)
            for b in range(4):
                results[a, b] = merged[count * b : count * (b + 1)]

        @pl.when(step == 1)
        def _():
            for a in (2, 3):
                for b in range(4):
                    spread(row_scr, a - 2, 8 + b - 2, results[a, b])

        @pl.when(step == 2)
        def _():
            for b in (0, 1):
                for a in range(4):
                    spread(col_scr, 2 + b, 8 + a - 2, results[a, b])

        @pl.when(step == 3)
        def _():
            for a in (0, 1):
                for b in range(4):
                    spread(row_scr, 2 + a, 8 + b + 2, results[a, b])

        @pl.when(step == 4)
        def _():
            for b in (2, 3):
                for a in range(4):
                    spread(col_scr, b - 2, 8 + a + 2, results[a, b])

    @pl.when(step == 4)
    def _():
        for c in range(2):
            for a in range(2):
                for h in range(2):
                    row_scr[2 * a + h, pl.ds(8 + OUT - 2 + c, 1), :] = col_scr[2 * (2 + c) + h, pl.ds(8 + a, 1), :]
                    row_scr[2 * (2 + a) + h, pl.ds(8 + c, 1), :] = col_scr[2 * c + h, pl.ds(8 + OUT - 2 + a, 1), :]
        for a in range(4):
            row_out[a] = both(row_scr, a, pl.ds(8, OUT)).astype(BF16)
        for copy in col_in:
            copy.wait()
        place = lax.broadcasted_iota(jnp.int32, (16, 2 * C), 0)
        for side, first in ((0, 0), (1, 14)):
            for r in range(2, OUT - 2):
                old = col_out[side, r].astype(F32)
                for c in range(2):
                    old = jnp.where(place == first + c, both(col_scr, 2 * side + c, pl.ds(8 + r, 1)), old)
                col_out[side, r] = old.astype(BF16)
        inside = pl.ds(2, OUT - 4)
        copies = [
            pltpu.make_async_copy(
                col_out.at[n, inside], out_ref.at[inside, pl.ds(at, 16), :], sem_out.at[n]
            )
            for n, at in enumerate((0, OUT - 16))
        ]
        copies += [
            pltpu.make_async_copy(row_out.at[pl.ds(2 * n, 2)], out_ref.at[pl.ds(at, 2)], sem_out.at[2 + n])
            for n, at in enumerate((0, OUT - 2))
        ]
        for copy in copies:
            copy.start()
        for copy in copies:
            copy.wait()


def border(tokens, ids, got, rel_index, bias_table, weights, inner):
    line = 4 * SIDE
    return pl.pallas_call(
        border_kernel,
        grid=(5,),
        out_shape=jax.ShapeDtypeStruct((OUT, OUT, 2 * C), BF16),
        in_specs=edge_specs()
        + [whole((STRIPS, SIDE), pltpu.SMEM)]
        + [whole(a.shape) for a in got]
        + [whole(rel_index.shape), whole(bias_table.shape)]
        + [whole(a.shape) for a in weights]
        + [pl.BlockSpec(memory_space=pl.ANY)],
        out_specs=pl.BlockSpec(memory_space=pl.ANY),
        input_output_aliases={15 + len(weights): 0},
        scratch_shapes=[
            pltpu.VMEM((VARIANTS, SPOTS, HEADS * SPOTS), F32),
            pltpu.VMEM((C, C), BF16),
            pltpu.VMEM((C, MLP), BF16),
            pltpu.VMEM((256, 128), F32),
            pltpu.VMEM((16 // GROUP, C, SPOTS * GROUP), BF16),
            pltpu.VMEM((16 * SPOTS, C), F32),
            pltpu.VMEM((4, 16, SPOTS, C), F32),
            pltpu.VMEM((4 * line + 64, C), F32),
            pltpu.VMEM((8 * STRIPS, SIDE), jnp.int32),
            pltpu.SMEM((8 * STRIPS, SIDE), jnp.int32),
            pltpu.SMEM((4, 16), jnp.int32),
            pltpu.VMEM((8, OUT + 16, C), F32),
            pltpu.VMEM((8, OUT + 16, C), F32),
            pltpu.VMEM((4, OUT, 2 * C), BF16),
            pltpu.VMEM((2, OUT, 16, 2 * C), BF16),
            pltpu.SemaphoreType.DMA,
            pltpu.SemaphoreType.DMA((2,)),
            pltpu.SemaphoreType.DMA((4,)),
        ],
        compiler_params=pltpu.CompilerParams(vmem_limit_bytes=56 * 1024 * 1024),
    )(tokens, tokens, tokens, tokens, ids, *got, rel_index, bias_table, *weights, inner)


def on_device(
    tokens, regions, rel_index, bias_table, norm1_gain, w_qkv, w_proj, norm2_gain, w_up, w_down, merge_gain, w_merge
):
    weights = (
        norm1_gain.reshape(1, C), w_qkv, w_proj, norm2_gain.reshape(1, C), w_up, w_down,
        merge_gain.reshape(1, 4 * C), w_merge,
    )
    ids, *messages = pack(tokens, regions)
    got = exchange(messages)
    inner = interior(tokens, ids, rel_index, bias_table, weights)
    return border(tokens, ids, got, rel_index, bias_table, weights, inner)


def solution(mesh):
    return jax.shard_map(
        on_device,
        mesh=mesh,
        in_specs=(P("row", "col", None), P("row", "col")) + (P(),) * 10,
        out_specs=P("row", "col", None),
        check_vma=False,
    )
```

```python
import functools

import jax
import jax.numpy as jnp
from jax import lax
from jax.experimental import pallas as pl
from jax.experimental.pallas import tpu as pltpu
from jax.sharding import PartitionSpec as P

C = 128
HEADS = 4
HD = 32
WIN = 8
SPOTS = WIN * WIN
MLP = 512
SIDE = 128
OUT = SIDE // 2
STRIPS = SIDE // 16
IDROWS = 16
EARLY = 3
LOG2E = 1.4426950408889634
QSCALE = HD ** (-0.5) * LOG2E
VARIANTS = 24
F32 = jnp.float32
BF16 = jnp.bfloat16
NT = (((1,), (1,)), ((), ()))
TN = (((0,), (0,)), ((), ()))


def layer_norm(values, gain):
    mean = jnp.mean(values, axis=-1, keepdims=True)
    centred = values - mean
    var = jnp.mean(centred * centred, axis=-1, keepdims=True)
    return centred * lax.rsqrt(var + 1e-05) * gain


def half_gelu(half):
    h = half.astype(BF16)
    c0 = jnp.asarray(2.0 * 0.7978845608028654, BF16)
    c1 = jnp.asarray(8.0 * 0.7978845608028654 * 0.044715, BF16)
    inner = h * (c0 + c1 * (h * h))
    return h + h * jnp.tanh(inner)


def prepare(rel_ref, table_ref, w_qkv_ref, w_up_ref, bias_scr, wvt_scr, wup_scr, pad_scr):
    wvt_scr[...] = w_qkv_ref[:, 2 * C :].astype(F32).T.astype(BF16)
    wup_scr[...] = w_up_ref[...] * jnp.asarray(0.5, BF16)
    pad_scr[...] = jnp.zeros_like(pad_scr)
    pad_scr[pl.ds(0, table_ref.shape[0]), pl.ds(0, HEADS)] = table_ref[...]
    table_a = pad_scr[pl.ds(0, 128), :].T
    table_b = pad_scr[pl.ds(128, 128), :].T
    pad_scr[pl.ds(0, SPOTS), pl.ds(0, SPOTS)] = rel_ref[...].astype(F32)
    rel_t = pad_scr[pl.ds(0, 128), :].T[:SPOTS, :].astype(jnp.int32)
    rel_t = jnp.where(lax.broadcasted_iota(jnp.int32, (SPOTS, 128), 1) < SPOTS, rel_t, pltpu.roll(rel_t, SPOTS, 1))
    low = rel_t < 128
    spot = jnp.where(low, rel_t, rel_t - 128)
    lane = lax.broadcasted_iota(jnp.int32, (SPOTS, 128), 1)
    halves = []
    for pair in range(HEADS // 2):
        per_head = []
        for head in (2 * pair, 2 * pair + 1):
            row_a = jnp.broadcast_to(table_a[head : head + 1, :], (SPOTS, 128))
            row_b = jnp.broadcast_to(table_b[head : head + 1, :], (SPOTS, 128))
            got_a = jnp.take_along_axis(row_a, spot, axis=1, mode="promise_in_bounds")
            got_b = jnp.take_along_axis(row_b, spot, axis=1, mode="promise_in_bounds")
            per_head.append(jnp.where(low, got_a, got_b))
        halves.append(jnp.where(lane < SPOTS, per_head[0], per_head[1]) * LOG2E)
    bias = jnp.concatenate(halves, axis=1)
    key_spot = lax.broadcasted_iota(jnp.int32, (SPOTS, 2 * 128), 0)
    query_spot = lax.broadcasted_iota(jnp.int32, (SPOTS, 2 * 128), 1) % SPOTS

    def label_of(spots, labels):
        right = (spots % WIN) >= WIN // 2
        lower = spots >= SPOTS // 2
        top = jnp.where(right, labels[0], 0)
        low_row = jnp.where(right, labels[2], labels[1])
        return jnp.where(lower, low_row, top)

    def variant(index, carry):
        labels = (index // 12, (index // 4) % 3, index % 4)
        same = label_of(key_spot, labels) == label_of(query_spot, labels)
        bias_scr[index] = jnp.where(same, bias, -1e30)
        return carry

    lax.fori_loop(0, VARIANTS, variant, 0)


def pattern(top_left, top_right, low_left, low_right):
    one = jnp.where(top_right == top_left, 0, 1)
    two = jnp.where(low_left == top_left, 0, jnp.where(low_left == top_right, 1, 2))
    three = jnp.where(
        low_right == top_left,
        0,
        jnp.where(low_right == top_right, 1, jnp.where(low_right == low_left, 2, 3)),
    )
    return one * 12 + two * 4 + three


def front(loads, store_att, variants, w, bias_scr, wvt_scr):
    normed = []
    for load in loads:
        normed.append(layer_norm(load(), w["g1"][...]).astype(BF16))
        yield
    normed = jnp.concatenate(normed, axis=0)
    qk = jnp.dot(normed, w["w_qkv"][:, : 2 * C], preferred_element_type=F32)
    vt = lax.dot_general(wvt_scr[...], normed, NT, preferred_element_type=F32).astype(BF16)
    yield
    lane = lax.broadcasted_iota(jnp.int32, (1, C), 1)
    n = len(loads)
    st, ot = {}, {}
    for i in range(n + 2 * LAG):
        if i < n:
            rows = slice(SPOTS * i, SPOTS * (i + 1))
            q = (qk[rows, :C] * QSCALE).astype(BF16)
            k = qk[rows, C:].astype(BF16)
            qm = jnp.concatenate([jnp.where(lane // HD == h, q, jnp.zeros_like(q)) for h in range(HEADS)], axis=0)
            st[i] = lax.dot_general(k, qm, NT, preferred_element_type=F32)
        at = i - LAG
        if 0 <= at < n:
            rows = slice(SPOTS * at, SPOTS * (at + 1))
            scores = st.pop(at) + bias_scr[variants[at]]
            top = jnp.max(scores, axis=0, keepdims=True)
            p = jnp.exp2((scores - top).astype(BF16))
            vw = jnp.concatenate([vt[:, rows], jnp.ones((16, SPOTS), BF16)], axis=0)
            ot[at] = jnp.dot(vw, p, preferred_element_type=F32)
        at = i - 2 * LAG
        if 0 <= at < n:
            got = ot.pop(at)
            inv = 1.0 / got[C : C + 1]
            store_att(
                at,
                jnp.concatenate(
                    [
                        got[HD * h : HD * (h + 1), SPOTS * h : SPOTS * (h + 1)]
                        * inv[:, SPOTS * h : SPOTS * (h + 1)]
                        for h in range(HEADS)
                    ],
                    axis=0,
                ).astype(BF16),
            )
        yield


def back(loads, load_att, stores, w, wup_scr):
    proj = lax.dot_general(load_att(), w["w_proj"][...], TN, preferred_element_type=F32)
    yield
    mids, second = [], []
    for i, load in enumerate(loads):
        mids.append(load() + proj[SPOTS * i : SPOTS * (i + 1)])
        second.append(layer_norm(mids[-1], w["g2"][...]).astype(BF16))
        yield
    up = jnp.dot(jnp.concatenate(second, axis=0), wup_scr[...], preferred_element_type=F32)
    yield
    wide = []
    for i in range(len(loads)):
        wide.append(half_gelu(up[SPOTS * i : SPOTS * (i + 1)]))
        yield
    down = jnp.dot(jnp.concatenate(wide, axis=0), w["w_down"][...], preferred_element_type=F32)
    yield
    for i, store in enumerate(stores):
        store(mids[i] + down[SPOTS * i : SPOTS * (i + 1)])
        yield


LAG = 2


def merge(load_parts, store, w):
    joined = jnp.concatenate(load_parts(), axis=1)
    normed = layer_norm(joined, w["gm"][...]).astype(BF16)
    yield
    out = jnp.dot(normed, w["w_merge"][...], preferred_element_type=F32)
    yield
    store(out.astype(BF16))


def drive(timed):
    events = []
    for number, (start, gap, gen) in enumerate(timed):
        for step in range(80):
            events.append((start + gap * step, number, gen))
    for _, _, gen in sorted(events, key=lambda e: (e[0], e[1])):
        next(gen, None)


NAMES = ("g1", "w_qkv", "w_proj", "g2", "w_up", "w_down", "gm", "w_merge")
GROUP = 8
FRONT_EVERY, FRONT_GAP = 20, 1
BACK_EVERY, BACK_GAP = 16, 0.8
MERGE_EVERY, MERGE_GAP, MERGE_AT = 1.0, 1.0, 50


def interior_kernel(first, total, x_ref, old_ref, ids_ref, rel_ref, table_ref, *refs):
    w = dict(zip(NAMES, refs[:8]))
    out_ref, bias_scr, wvt_scr, wup_scr, pad_scr, att_scr, blk_scr = refs[-7:]
    step = pl.program_id(0)
    count = SIDE // WIN - 1

    @pl.when(step == 0)
    def _():
        prepare(rel_ref, table_ref, w["w_qkv"], w["w_up"], bias_scr, wvt_scr, wup_scr, pad_scr)
        blk_scr[...] = jnp.zeros_like(blk_scr)

    upper = jnp.minimum(first + step, count - 1) // 2
    lower = jnp.minimum(first + step + 1, count) // 2

    def loader(ref, j):
        return lambda: jnp.concatenate([ref[y, pl.ds(WIN * j + 4, WIN), :] for y in range(WIN)], axis=0)

    def variant(j):
        left, right = 16 * (j // 2), 16 * ((j + 1) // 2)
        return pattern(ids_ref[upper, left], ids_ref[upper, right], ids_ref[lower, left], ids_ref[lower, right])

    def store_att(g):
        def store(i, value):
            att_scr[g, :, pl.ds(SPOTS * i, SPOTS)] = value

        return store

    def store_block(j):
        def store(value):
            for y in range(WIN):
                blk_scr[y, pl.ds(WIN * j + 4, WIN), :] = value[WIN * y : WIN * (y + 1)]

        return store

    groups = [list(range(at, min(at + GROUP, count))) for at in range(0, count, GROUP)]

    def fronts():
        return [
            (
                FRONT_EVERY * g,
                FRONT_GAP,
                front([loader(x_ref, j) for j in js], store_att(g), [variant(j) for j in js], w, bias_scr, wvt_scr),
            )
            for g, js in enumerate(groups)
        ]

    def backs():
        return [
            (
                BACK_EVERY * g,
                BACK_GAP,
                back(
                    [loader(old_ref, j) for j in js],
                    lambda g=g, js=js: att_scr[g, :, : SPOTS * len(js)],
                    [store_block(j) for j in js],
                    w,
                    wup_scr,
                ),
            )
            for g, js in enumerate(groups)
        ]

    def merges():
        def parts(a):
            return lambda: [blk_scr[2 * a + dy, pl.ds(dx, OUT, stride=2), :] for dx in range(2) for dy in range(2)]

        def store(a):
            def put(value):
                out_ref[a] = value

            return put

        return [(MERGE_AT + MERGE_EVERY * a, MERGE_GAP, merge(parts(a), store(a), w)) for a in range(4)]

    @pl.when(step == 0)
    def _():
        drive(fronts())

    @pl.when((step > 0) & (step < total))
    def _():
        drive(backs() + fronts() + merges())

    @pl.when(step == total)
    def _():
        drive(backs() + merges())


def whole(shape, space=pltpu.VMEM):
    return pl.BlockSpec(shape, lambda i: (0,) * len(shape), memory_space=space)


def interior(tokens, ids, rel_index, bias_table, weights, first, total, before=None, after=None):
    groups = pl.cdiv(SIDE // WIN - 1, GROUP)
    strip = (pl.Element(WIN), pl.Element(SIDE), pl.Element(C))
    extra = () if before is None else (before, after)
    args = (tokens, tokens, ids, rel_index, bias_table, *weights, *extra)
    return pl.pallas_call(
        functools.partial(interior_kernel, first, total),
        grid=(total + 1,),
        out_shape=jax.ShapeDtypeStruct((OUT, OUT, 2 * C), BF16),
        in_specs=[
            pl.BlockSpec(strip, lambda i: (WIN * (first + jnp.minimum(i, total - 1)) + 4, 0, 0)),
            pl.BlockSpec(strip, lambda i: (WIN * (first + jnp.maximum(i - 1, 0)) + 4, 0, 0)),
            whole((STRIPS, SIDE), pltpu.SMEM),
            whole(rel_index.shape),
            whole(bias_table.shape),
        ]
        + [whole(a.shape) for a in weights]
        + [pl.BlockSpec(memory_space=pl.ANY) for _ in extra],
        out_specs=pl.BlockSpec(
            (pl.Element(4), pl.Element(OUT), pl.Element(2 * C)),
            lambda i: (4 * (first + jnp.maximum(i - 1, 0)) + 2, 0, 0),
        ),
        input_output_aliases={} if before is None else {len(args) - 2: 0},
        scratch_shapes=[
            pltpu.VMEM((VARIANTS, SPOTS, HEADS * SPOTS), F32),
            pltpu.VMEM((C, C), BF16),
            pltpu.VMEM((C, MLP), BF16),
            pltpu.VMEM((256, 128), F32),
            pltpu.VMEM((groups, C, SPOTS * GROUP), BF16),
            pltpu.VMEM((WIN, SIDE, C), F32),
        ],
        compiler_params=pltpu.CompilerParams(vmem_limit_bytes=56 * 1024 * 1024),
    )(*args)


LINE = 4 * SIDE
BAND = 4 * (SIDE + 8)


def row_specs():
    return [
        pl.BlockSpec((4, SIDE, C), lambda i: (0, 0, 0)),
        pl.BlockSpec((4, SIDE, C), lambda i: (SIDE // 4 - 1, 0, 0)),
    ]


def col_specs():
    return [
        pl.BlockSpec((SIDE, 8, C), lambda i: (0, 0, 0)),
        pl.BlockSpec((SIDE, 8, C), lambda i: (0, SIDE // 8 - 1, 0)),
    ]


def pack_rows_kernel(top_ref, bottom_ref, regions_ref, ids_ref, *messages):
    ids = regions_ref[pl.ds(0, STRIPS, stride=16), :]
    ids_ref[...] = ids
    coded = jnp.concatenate([ids, ids], axis=0).astype(F32).astype(BF16)
    for out, source in zip(messages, (top_ref, bottom_ref)):
        for y in range(4):
            out[pl.ds(SIDE * y, SIDE), :] = source[y].astype(BF16)
        out[pl.ds(LINE, IDROWS), :] = coded


def pack_rows(tokens, regions):
    line = jax.ShapeDtypeStruct((LINE + IDROWS, C), BF16)
    shapes = [jax.ShapeDtypeStruct((STRIPS, SIDE), jnp.int32), line, line]
    return pl.pallas_call(
        pack_rows_kernel,
        grid=(1,),
        out_shape=shapes,
        in_specs=row_specs() + [whole((SIDE, SIDE))],
        out_specs=[whole(a.shape) for a in shapes],
    )(tokens, tokens, regions)


def pack_cols_kernel(left_ref, right_ref, above_ref, below_ref, ids_ref, after_ref, to_left, to_right, token_ref, band_scr, row_scr):
    token_ref[...] = jnp.zeros_like(token_ref)
    row_scr[0] = above_ref[pl.ds(0, LINE), :].astype(F32)
    row_scr[1] = below_ref[pl.ds(0, LINE), :].astype(F32)
    ids = ids_ref[...]
    own = jnp.concatenate([ids, ids], axis=0).astype(F32).astype(BF16)
    for out, source, at, far in ((to_left, left_ref, 0, 0), (to_right, right_ref, 4, SIDE - 4)):
        for y in range(4):
            band_scr[pl.ds(4 * y, 4), :] = row_scr[0, pl.ds(SIDE * y + far, 4), :]
            band_scr[pl.ds(4 * (SIDE + 4 + y), 4), :] = row_scr[1, pl.ds(SIDE * y + far, 4), :]
        for r in range(SIDE):
            band_scr[pl.ds(4 * (r + 4), 4), :] = source[r, pl.ds(at, 4), :]
        out[pl.ds(0, BAND), :] = band_scr[...].astype(BF16)
        out[pl.ds(BAND, IDROWS), :] = above_ref[pl.ds(LINE, IDROWS), :]
        out[pl.ds(BAND + IDROWS, IDROWS), :] = own
        out[pl.ds(BAND + 2 * IDROWS, IDROWS), :] = below_ref[pl.ds(LINE, IDROWS), :]


def pack_cols(tokens, above, below, ids, after):
    band = jax.ShapeDtypeStruct((BAND + 3 * IDROWS, C), BF16)
    token = jax.ShapeDtypeStruct((8, C), F32)
    return pl.pallas_call(
        pack_cols_kernel,
        grid=(1,),
        out_shape=[band, band, token],
        in_specs=col_specs()
        + [whole(above.shape), whole(below.shape), whole(ids.shape), pl.BlockSpec(memory_space=pl.ANY)],
        out_specs=[whole(band.shape), whole(band.shape), whole(token.shape)],
        scratch_shapes=[pltpu.VMEM((BAND, C), F32), pltpu.VMEM((2, LINE, C), F32)],
    )(tokens, tokens, above, below, ids, after)


def moved(value, axis, by):
    size = lax.axis_size(axis)
    return lax.ppermute(value, axis, [(i, (i + by) % size) for i in range(size)])


def gather_border(edges, got, x_scr, msg_scr):
    top, bottom, left, right = edges
    line = 4 * SIDE
    for n in range(2):
        msg_scr[pl.ds(line * n, line), :] = got[n][pl.ds(0, line), :].astype(F32)
        msg_scr[pl.ds(2 * line + BAND * n, BAND), :] = got[2 + n][pl.ds(0, BAND), :].astype(F32)

    def row_of(n):
        return lambda y, at, size: msg_scr[pl.ds(line * n + SIDE * y + at, size), :]

    def col_of(n):
        return lambda r, at, size: msg_scr[pl.ds(2 * line + BAND * n + 4 * (r + 4) + at, size), :]

    def own(ref):
        return lambda y, at, size: ref[y, pl.ds(at, size), :]

    above, below, from_left, from_right = row_of(0), row_of(1), col_of(0), col_of(1)
    for t in range(16):
        for y in range(8):
            spot = WIN * y
            side, at = (above, y) if y < 4 else (own(top), y - 4)
            if t == 0:
                edge = from_left(y - 4, 0, 4)
                x_scr[0, t, pl.ds(spot, 4), :] = edge
                x_scr[0, t, pl.ds(spot + 4, 4), :] = side(at, 0, 4)
            else:
                x_scr[0, t, pl.ds(spot, 8), :] = side(at, 8 * t - 4, 8)
            side, at = (own(bottom), y) if y < 4 else (below, y - 4)
            if t == 15:
                edge = from_right(124 + y, 0, 4)
                x_scr[2, t, pl.ds(spot, 4), :] = side(at, 124, 4)
                x_scr[2, t, pl.ds(spot + 4, 4), :] = edge
            else:
                x_scr[2, t, pl.ds(spot, 8), :] = side(at, 8 * t + 4, 8)
            r = 8 * t - 4 + y
            x_scr[1, t, pl.ds(spot, 4), :] = above(y, 124, 4) if r < 0 else own(right)(r, 4, 4)
            x_scr[1, t, pl.ds(spot + 4, 4), :] = from_right(r, 0, 4)
            r = 8 * t + 4 + y
            x_scr[3, t, pl.ds(spot, 4), :] = from_left(r, 0, 4)
            x_scr[3, t, pl.ds(spot + 4, 4), :] = below(r - SIDE, 0, 4) if r >= SIDE else own(left)(r, 0, 4)


def border_patterns(id_at, var_smem):
    for t in range(16):
        before = ((t + 1) // 2 - 1, t // 2)
        after = (t // 2, (t + 1) // 2)
        pairs = (((-1, 0), before), (before, (7, 8)), ((7, 8), after), (after, (-1, 0)))
        for s, (rs, cs) in enumerate(pairs):
            var_smem[s, t] = pattern(id_at(rs[0], cs[0]), id_at(rs[0], cs[1]), id_at(rs[1], cs[0]), id_at(rs[1], cs[1]))


def border_kernel(*refs):
    edges, own_ids, got = refs[:4], refs[4], refs[5:9]
    rel_ref, table_ref = refs[9:11]
    w = dict(zip(NAMES, refs[11:19]))
    inner_ref, out_ref = refs[19:21]
    (bias_scr, wvt_scr, wup_scr, pad_scr, att_scr, blk_scr, x_scr, msg_scr, idv_scr, ids_smem, var_smem, row_scr,
     col_scr, row_out, col_out, sem_ids, sem_in, sem_out) = refs[21:]
    step = pl.program_id(0)
    count = 16
    col_in = [
        pltpu.make_async_copy(inner_ref.at[:, pl.ds(at, 16), :], col_out.at[n], sem_in.at[n])
        for n, at in enumerate((0, OUT - 16))
    ]

    @pl.when(step == 0)
    def _():
        for copy in col_in:
            copy.start()
        places = [(0, LINE), (1, LINE)]
        places += [(2 + side, BAND + IDROWS * m) for side in range(2) for m in range(3)]
        for n, (source, first) in enumerate(places):
            idv_scr[pl.ds(STRIPS * n, STRIPS), :] = (
                got[source][pl.ds(first, IDROWS), :].astype(F32)[:STRIPS].astype(jnp.int32)
            )
        ids_copy = pltpu.make_async_copy(idv_scr, ids_smem, sem_ids)
        ids_copy.start()
        gather_border(edges, got, x_scr, msg_scr)
        prepare(rel_ref, table_ref, w["w_qkv"], w["w_up"], bias_scr, wvt_scr, wup_scr, pad_scr)
        ids_copy.wait()
        places = {(-1, 0): 0, (1, 0): 1, (-1, -1): 2, (0, -1): 3, (1, -1): 4, (-1, 1): 5, (0, 1): 6, (1, 1): 7}

        def id_at(m, n):
            where = (-1 if m < 0 else int(m >= STRIPS), -1 if n < 0 else int(n >= STRIPS))
            m, n = m % STRIPS, n % STRIPS
            if where == (0, 0):
                return own_ids[m, 16 * n]
            return ids_smem[STRIPS * places[where] + m, 16 * n]

        border_patterns(id_at, var_smem)

    groups = [list(range(at, at + GROUP)) for at in range(0, count, GROUP)]

    def store_att(g):
        def store(i, value):
            att_scr[g, :, pl.ds(SPOTS * i, SPOTS)] = value

        return store

    def store_block(t):
        def store(value):
            blk_scr[pl.ds(SPOTS * t, SPOTS), :] = value

        return store

    def fronts():
        return [
            (
                FRONT_EVERY * g,
                FRONT_GAP,
                front(
                    [lambda t=t: x_scr[step, t] for t in ts],
                    store_att(g),
                    [var_smem[step, t] for t in ts],
                    w,
                    bias_scr,
                    wvt_scr,
                ),
            )
            for g, ts in enumerate(groups)
        ]

    def backs():
        return [
            (
                BACK_EVERY * g,
                BACK_GAP,
                back(
                    [lambda t=t: x_scr[step - 1, t] for t in ts],
                    lambda g=g: att_scr[g],
                    [store_block(t) for t in ts],
                    w,
                    wup_scr,
                ),
            )
            for g, ts in enumerate(groups)
        ]

    @pl.when(step == 0)
    def _():
        drive(fronts())

    @pl.when((step > 0) & (step < 4))
    def _():
        drive(backs() + fronts())

    @pl.when(step == 4)
    def _():
        drive(backs())

    def spread(scr, at, first, value):
        for half in range(2):
            scr[2 * at + half, pl.ds(first, count, stride=4), :] = value[:, C * half : C * (half + 1)]

    def both(scr, at, rows):
        return jnp.concatenate([scr[2 * at + half, rows, :] for half in range(2)], axis=1)

    @pl.when(step > 0)
    def _():
        results = {}
        for a in range(4):
            joined = []
            for dx in range(2):
                for dy in range(2):
                    joined.append(
                        jnp.concatenate(
                            [
                                blk_scr[pl.ds((2 * a + dy) * WIN + 2 * b + dx, count, stride=SPOTS), :]
                                for b in range(4)
                            ],
                            axis=0,
                        )
                    )
            normed = layer_norm(jnp.concatenate(joined, axis=1), w["gm"][...]).astype(BF16)
            merged = jnp.dot(normed, w["w_merge"][...], preferred_element_type=F32)
            for b in range(4):
                results[a, b] = merged[count * b : count * (b + 1)]

        @pl.when(step == 1)
        def _():
            for a in (2, 3):
                for b in range(4):
                    spread(row_scr, a - 2, 8 + b - 2, results[a, b])

        @pl.when(step == 2)
        def _():
            for b in (0, 1):
                for a in range(4):
                    spread(col_scr, 2 + b, 8 + a - 2, results[a, b])

        @pl.when(step == 3)
        def _():
            for a in (0, 1):
                for b in range(4):
                    spread(row_scr, 2 + a, 8 + b + 2, results[a, b])

        @pl.when(step == 4)
        def _():
            for b in (2, 3):
                for a in range(4):
                    spread(col_scr, b - 2, 8 + a + 2, results[a, b])

    @pl.when(step == 4)
    def _():
        for c in range(2):
            for a in range(2):
                for h in range(2):
                    row_scr[2 * a + h, pl.ds(8 + OUT - 2 + c, 1), :] = col_scr[2 * (2 + c) + h, pl.ds(8 + a, 1), :]
                    row_scr[2 * (2 + a) + h, pl.ds(8 + c, 1), :] = col_scr[2 * c + h, pl.ds(8 + OUT - 2 + a, 1), :]
        for a in range(4):
            row_out[a] = both(row_scr, a, pl.ds(8, OUT)).astype(BF16)
        for copy in col_in:
            copy.wait()
        place = lax.broadcasted_iota(jnp.int32, (16, 2 * C), 0)
        for side, first in ((0, 0), (1, 14)):
            for r in range(2, OUT - 2):
                old = col_out[side, r].astype(F32)
                for c in range(2):
                    old = jnp.where(place == first + c, both(col_scr, 2 * side + c, pl.ds(8 + r, 1)), old)
                col_out[side, r] = old.astype(BF16)
        inside = pl.ds(2, OUT - 4)
        copies = [
            pltpu.make_async_copy(
                col_out.at[n, inside], out_ref.at[inside, pl.ds(at, 16), :], sem_out.at[n]
            )
            for n, at in enumerate((0, OUT - 16))
        ]
        copies += [
            pltpu.make_async_copy(row_out.at[pl.ds(2 * n, 2)], out_ref.at[pl.ds(at, 2)], sem_out.at[2 + n])
            for n, at in enumerate((0, OUT - 2))
        ]
        for copy in copies:
            copy.start()
        for copy in copies:
            copy.wait()


def border(tokens, ids, got, rel_index, bias_table, weights, inner):
    return pl.pallas_call(
        border_kernel,
        grid=(5,),
        out_shape=jax.ShapeDtypeStruct((OUT, OUT, 2 * C), BF16),
        in_specs=row_specs()
        + col_specs()
        + [whole((STRIPS, SIDE), pltpu.SMEM)]
        + [whole(a.shape) for a in got]
        + [whole(rel_index.shape), whole(bias_table.shape)]
        + [whole(a.shape) for a in weights]
        + [pl.BlockSpec(memory_space=pl.ANY)],
        out_specs=pl.BlockSpec(memory_space=pl.ANY),
        input_output_aliases={11 + len(weights): 0},
        scratch_shapes=[
            pltpu.VMEM((VARIANTS, SPOTS, HEADS * SPOTS), F32),
            pltpu.VMEM((C, C), BF16),
            pltpu.VMEM((C, MLP), BF16),
            pltpu.VMEM((256, 128), F32),
            pltpu.VMEM((16 // GROUP, C, SPOTS * GROUP), BF16),
            pltpu.VMEM((16 * SPOTS, C), F32),
            pltpu.VMEM((4, 16, SPOTS, C), F32),
            pltpu.VMEM((2 * LINE + 2 * BAND, C), F32),
            pltpu.VMEM((8 * STRIPS, SIDE), jnp.int32),
            pltpu.SMEM((8 * STRIPS, SIDE), jnp.int32),
            pltpu.SMEM((4, 16), jnp.int32),
            pltpu.VMEM((8, OUT + 16, C), F32),
            pltpu.VMEM((8, OUT + 16, C), F32),
            pltpu.VMEM((4, OUT, 2 * C), BF16),
            pltpu.VMEM((2, OUT, 16, 2 * C), BF16),
            pltpu.SemaphoreType.DMA,
            pltpu.SemaphoreType.DMA((2,)),
            pltpu.SemaphoreType.DMA((4,)),
        ],
        compiler_params=pltpu.CompilerParams(vmem_limit_bytes=56 * 1024 * 1024),
    )(tokens, tokens, tokens, tokens, ids, *got, rel_index, bias_table, *weights, inner)


def on_device(
    tokens, regions, rel_index, bias_table, norm1_gain, w_qkv, w_proj, norm2_gain, w_up, w_down, merge_gain, w_merge
):
    weights = (
        norm1_gain.reshape(1, C), w_qkv, w_proj, norm2_gain.reshape(1, C), w_up, w_down,
        merge_gain.reshape(1, 4 * C), w_merge,
    )
    ids, top, bottom = pack_rows(tokens, regions)
    above, below = moved(bottom, "row", 1), moved(top, "row", -1)
    inner = interior(tokens, ids, rel_index, bias_table, weights, 0, EARLY)
    to_left, to_right, token = pack_cols(tokens, above, below, ids, inner)
    from_left, from_right = moved(to_right, "col", 1), moved(to_left, "col", -1)
    inner = interior(
        tokens, ids, rel_index, bias_table, weights, EARLY, SIDE // WIN - 1 - EARLY, before=inner, after=token
    )
    return border(
        tokens, ids, (above, below, from_left, from_right), rel_index, bias_table, weights, inner
    )


def solution(mesh):
    return jax.shard_map(
        on_device,
        mesh=mesh,
        in_specs=(P("row", "col", None), P("row", "col")) + (P(),) * 10,
        out_specs=P("row", "col", None),
        check_vma=False,
    )
```

```python
import functools

import jax
import jax.numpy as jnp
from jax import lax
from jax.experimental import pallas as pl
from jax.experimental.pallas import tpu as pltpu
from jax.sharding import PartitionSpec as P

C = 128
HEADS = 4
HD = 32
WIN = 8
SPOTS = WIN * WIN
MLP = 512
SIDE = 128
OUT = SIDE // 2
STRIPS = SIDE // 16
IDROWS = 16
EARLY = 3
LOG2E = 1.4426950408889634
QSCALE = HD ** (-0.5) * LOG2E
VARIANTS = 24
F32 = jnp.float32
BF16 = jnp.bfloat16
NT = (((1,), (1,)), ((), ()))
TN = (((0,), (0,)), ((), ()))


def layer_norm(values, gain):
    mean = jnp.mean(values, axis=-1, keepdims=True)
    centred = values - mean
    var = jnp.mean(centred * centred, axis=-1, keepdims=True)
    return centred * lax.rsqrt(var + 1e-05) * gain


def half_gelu(half):
    h = half.astype(BF16)
    c0 = jnp.asarray(2.0 * 0.7978845608028654, BF16)
    c1 = jnp.asarray(8.0 * 0.7978845608028654 * 0.044715, BF16)
    inner = h * (c0 + c1 * (h * h))
    return h + h * jnp.tanh(inner)


def prepare_weights(table_ref, w_qkv_ref, w_up_ref, wvt_scr, wup_scr, pad_scr):
    wvt_scr[...] = w_qkv_ref[:, 2 * C :].astype(F32).T.astype(BF16)
    wup_scr[...] = w_up_ref[...] * jnp.asarray(0.5, BF16)
    pad_scr[...] = jnp.zeros_like(pad_scr)
    rest = table_ref.shape[1] - 128
    pad_scr[pl.ds(128, HEADS), :] = table_ref[:, :128]
    pad_scr[pl.ds(136, HEADS), pl.ds(0, rest)] = table_ref[:, 128:]


def from_table(rel, head, pad_scr):
    low = rel < 128
    spot = jnp.where(low, rel, rel - 128)
    got = []
    for first in (128, 136):
        row = jnp.broadcast_to(pad_scr[pl.ds(first + head, 1), :], rel.shape)
        got.append(jnp.take_along_axis(row, spot, axis=1, mode="promise_in_bounds"))
    return jnp.where(low, got[0], got[1]) * LOG2E


def fill_variants(bias_scr, first, bias, key_quarter, query_quarter):
    def label_of(quarter, labels):
        return jnp.where(
            quarter == 0, 0, jnp.where(quarter == 1, labels[0], jnp.where(quarter == 2, labels[1], labels[2]))
        )

    for one in range(2):
        for two in (0, 1, 2) if one else (0, 2):
            for three in range(4):
                if (three == 1 and not one) or (three == 2 and two != 2):
                    continue
                same = label_of(key_quarter, (one, two, three)) == label_of(query_quarter, (one, two, three))
                bias_scr[first + one * 12 + two * 4 + three] = jnp.where(same, bias, -1e30)


def prepare(rel_ref, table_ref, w_qkv_ref, w_up_ref, bias_scr, wvt_scr, wup_scr, pad_scr):
    prepare_weights(table_ref, w_qkv_ref, w_up_ref, wvt_scr, wup_scr, pad_scr)
    pad_scr[pl.ds(0, SPOTS), pl.ds(0, SPOTS)] = rel_ref[...].astype(F32)
    rel_t = pad_scr[pl.ds(0, 128), :].T[:SPOTS, :].astype(jnp.int32)
    lane = lax.broadcasted_iota(jnp.int32, (SPOTS, 128), 1)
    rel_t = jnp.where(lane < SPOTS, rel_t, pltpu.roll(rel_t, SPOTS, 1))
    halves = []
    for pair in range(HEADS // 2):
        per_head = [from_table(rel_t, head, pad_scr) for head in (2 * pair, 2 * pair + 1)]
        halves.append(jnp.where(lane < SPOTS, per_head[0], per_head[1]))

    def quarter(spots):
        return spots // 32 * 2 + spots % WIN // 4

    fill_variants(
        bias_scr,
        0,
        jnp.concatenate(halves, axis=1),
        quarter(lax.broadcasted_iota(jnp.int32, (SPOTS, 1), 0)),
        quarter(lax.broadcasted_iota(jnp.int32, (1, 2 * 128), 1) % SPOTS),
    )


def border_spot(strip, spot):
    if strip in (0, 2):
        return (spot + 32 * (strip == 0)) % SPOTS
    half, y, x = spot // 32, spot % 32 // 4, spot % 4
    return y * WIN + (half if strip == 1 else 1 - half) * 4 + x


def border_quarter(strip, spots):
    half = spots // 32
    if strip == 0:
        return (1 - half) * 2 + spots % WIN // 4
    if strip == 2:
        return half * 2 + spots % WIN // 4
    return spots % 32 // 16 * 2 + (half if strip == 1 else 1 - half)


def prepare_border(rel_ref, table_ref, w_qkv_ref, w_up_ref, bias_scr, wvt_scr, wup_scr, pad_scr, turn_scr):
    prepare_weights(table_ref, w_qkv_ref, w_up_ref, wvt_scr, wup_scr, pad_scr)
    lane = lax.broadcasted_iota(jnp.int32, (SPOTS, 128), 1)
    turn_scr[...] = jnp.zeros_like(turn_scr)
    for strip in range(4):
        for at in range(0, SPOTS, 4):
            pad_scr[pl.ds(at, 4), pl.ds(0, SPOTS)] = rel_ref[pl.ds(border_spot(strip, at), 4), :].astype(F32)
        turn_scr[...] = pad_scr[pl.ds(0, 128), :].T
        rel_t = jnp.concatenate(
            [turn_scr[pl.ds(border_spot(strip, at), 4), :] for at in range(0, SPOTS, 4)], axis=0
        )
        rel_t = jnp.where(lane < 32, rel_t, 0.0)
        rel_t = rel_t + pltpu.roll(rel_t, 32, 1)
        rel_t = (rel_t + pltpu.roll(rel_t, 64, 1)).astype(jnp.int32)
        bias = from_table(rel_t, 0, pad_scr)
        for head in range(1, HEADS):
            bias = jnp.where(lane // 32 == head, from_table(rel_t, head, pad_scr), bias)
        fill_variants(
            bias_scr,
            VARIANTS * strip,
            bias,
            border_quarter(strip, lax.broadcasted_iota(jnp.int32, (SPOTS, 1), 0)),
            border_quarter(strip, lax.broadcasted_iota(jnp.int32, (1, 128), 1) % 32),
        )


def pattern(top_left, top_right, low_left, low_right):
    one = jnp.where(top_right == top_left, 0, 1)
    two = jnp.where(low_left == top_left, 0, jnp.where(low_left == top_right, 1, 2))
    three = jnp.where(
        low_right == top_left,
        0,
        jnp.where(low_right == top_right, 1, jnp.where(low_right == low_left, 2, 3)),
    )
    return one * 12 + two * 4 + three


def front(loads, store_att, variants, w, bias_scr, wvt_scr, base, nrm_scr, q_scr, k_scr, vt_scr, nq=SPOTS):
    for i, load in enumerate(loads):
        nrm_scr[pl.ds(base + SPOTS * i, SPOTS), :] = layer_norm(load(), w["g1"][...]).astype(BF16)
        yield
    size = SPOTS * len(loads)
    for at in range(0, size, QPIECE):
        piece = min(QPIECE, size - at)
        rows = pl.ds(base + at, piece)
        qk = jnp.dot(nrm_scr[rows, :], w["w_qkv"][:, : 2 * C], preferred_element_type=F32)
        for i in range(0, piece, SPOTS):
            part = qk[i : i + SPOTS]
            q_scr[pl.ds(base + at + i, SPOTS), :] = (part[:, :C] * QSCALE).astype(BF16)
            k_scr[pl.ds(base + at + i, SPOTS), :] = part[:, C:].astype(BF16)
        yield
    for at in range(0, size, 256):
        wide = min(256, size - at)
        vt_scr[:, pl.ds(base + at, wide)] = lax.dot_general(
            wvt_scr[...], nrm_scr[pl.ds(base + at, wide), :], NT, preferred_element_type=F32
        ).astype(BF16)
    yield
    lane = lax.broadcasted_iota(jnp.int32, (1, C), 1)
    n = len(loads)
    st, ot = {}, {}
    for i in range(n + 2 * LAG):
        if i < n:
            rows = pl.ds(base + SPOTS * i, SPOTS)
            q = q_scr[pl.ds(base + SPOTS * i, nq), :]
            k = k_scr[rows, :]
            qm = jnp.concatenate([jnp.where(lane // HD == h, q, jnp.zeros_like(q)) for h in range(HEADS)], axis=0)
            st[i] = lax.dot_general(k, qm, NT, preferred_element_type=F32)
        at = i - LAG
        if 0 <= at < n:
            rows = slice(SPOTS * at, SPOTS * (at + 1))
            scores = st.pop(at) + bias_scr[variants[at]]
            top = jnp.max(scores, axis=0, keepdims=True)
            p = jnp.exp2((scores - top).astype(BF16))
            vw = jnp.concatenate([vt_scr[:, pl.ds(base + SPOTS * at, SPOTS)], jnp.ones((16, SPOTS), BF16)], axis=0)
            ot[at] = jnp.dot(vw, p, preferred_element_type=F32)
        at = i - 2 * LAG
        if 0 <= at < n:
            got = ot.pop(at)
            inv = 1.0 / got[C : C + 1]
            store_att(
                at,
                jnp.concatenate(
                    [
                        got[HD * h : HD * (h + 1), nq * h : nq * (h + 1)]
                        * inv[:, nq * h : nq * (h + 1)]
                        for h in range(HEADS)
                    ],
                    axis=0,
                ).astype(BF16),
            )
        yield


def back(loads, load_att, stores, w, wup_scr, base, mid_scr, sec_scr, wide_scr, nq=SPOTS):
    size = nq * len(loads)
    proj = lax.dot_general(load_att(), w["w_proj"][...], TN, preferred_element_type=F32)
    yield
    for i, load in enumerate(loads):
        rows = pl.ds(base + nq * i, nq)
        mid = load() + proj[nq * i : nq * (i + 1)]
        mid_scr[rows, :] = mid
        sec_scr[rows, :] = layer_norm(mid, w["g2"][...]).astype(BF16)
        yield
    for at in range(0, size, PIECE):
        piece = min(PIECE, size - at)
        up = jnp.dot(sec_scr[pl.ds(base + at, piece), :], wup_scr[...], preferred_element_type=F32)
        yield
        for i in range(0, piece, 32):
            wide_scr[pl.ds(base + at + i, 32), :] = half_gelu(up[i : i + 32])
            if i % 64:
                yield
    down = jnp.dot(wide_scr[pl.ds(base, size), :], w["w_down"][...], preferred_element_type=F32)
    yield
    for i, store in enumerate(stores):
        store(mid_scr[pl.ds(base + nq * i, nq), :] + down[nq * i : nq * (i + 1)])
        yield


PIECE = 256
QPIECE = 256
LAG = 1


def merge(load_parts, store, w):
    joined = jnp.concatenate(load_parts(), axis=1)
    normed = layer_norm(joined, w["gm"][...]).astype(BF16)
    yield
    out = jnp.dot(normed, w["w_merge"][...], preferred_element_type=F32)
    yield
    store(out.astype(BF16))


def drive(timed):
    events = []
    for number, (start, gap, gen) in enumerate(timed):
        for step in range(80):
            events.append((start + gap * step, number, gen))
    for _, _, gen in sorted(events, key=lambda e: (e[0], e[1])):
        next(gen, None)


NAMES = ("g1", "w_qkv", "w_proj", "g2", "w_up", "w_down", "gm", "w_merge")
GROUP = 8
FRONT_AT = 0
FRONT_EVERY, FRONT_GAP = 20, 1
BACK_EVERY, BACK_GAP = 16, 0.8
BORDER_FRONT_EVERY, BORDER_BACK_EVERY = 10, 12
MERGE_EVERY, MERGE_GAP, MERGE_AT = 1.0, 1.0, 50


def interior_kernel(first, total, x_ref, old_ref, ids_ref, rel_ref, table_ref, *refs):
    w = dict(zip(NAMES, refs[:8]))
    out_ref = refs[-14]
    (bias_scr, wvt_scr, wup_scr, pad_scr, att_scr, blk_scr, nrm_scr, q_scr, k_scr, vt_scr, mid_scr, sec_scr, wide_scr) = refs[-13:]
    step = pl.program_id(0)
    count = SIDE // WIN - 1

    @pl.when(step == 0)
    def _():
        prepare(rel_ref, table_ref, w["w_qkv"], w["w_up"], bias_scr, wvt_scr, wup_scr, pad_scr)
        blk_scr[...] = jnp.zeros_like(blk_scr)

    upper = jnp.minimum(first + step, count - 1) // 2
    lower = jnp.minimum(first + step + 1, count) // 2

    def loader(ref, j):
        return lambda: jnp.concatenate([ref[y, pl.ds(WIN * j + 4, WIN), :] for y in range(WIN)], axis=0)

    def variant(j):
        left, right = 16 * (j // 2), 16 * ((j + 1) // 2)
        return pattern(ids_ref[upper, left], ids_ref[upper, right], ids_ref[lower, left], ids_ref[lower, right])

    def store_att(g):
        def store(i, value):
            att_scr[g, :, pl.ds(SPOTS * i, SPOTS)] = value

        return store

    def store_block(j):
        def store(value):
            for y in range(WIN):
                blk_scr[y, pl.ds(WIN * j + 4, WIN), :] = value[WIN * y : WIN * (y + 1)]

        return store

    groups = [list(range(at, min(at + GROUP, count))) for at in range(0, count, GROUP)]

    def fronts():
        return [
            (
                FRONT_AT + FRONT_EVERY * g,
                FRONT_GAP,
                front([loader(x_ref, j) for j in js], store_att(g), [variant(j) for j in js], w, bias_scr, wvt_scr, SPOTS * js[0], nrm_scr, q_scr, k_scr, vt_scr),
            )
            for g, js in enumerate(groups)
        ]

    def backs():
        return [
            (
                BACK_EVERY * g,
                BACK_GAP,
                back(
                    [loader(old_ref, j) for j in js],
                    lambda g=g, js=js: att_scr[g, :, : SPOTS * len(js)],
                    [store_block(j) for j in js],
                    w,
                    wup_scr,
                    SPOTS * js[0],
                    mid_scr,
                    sec_scr,
                    wide_scr,
                ),
            )
            for g, js in enumerate(groups)
        ]

    def merges():
        def parts(a):
            return lambda: [blk_scr[2 * a + dy, pl.ds(dx, OUT, stride=2), :] for dx in range(2) for dy in range(2)]

        def store(a):
            def put(value):
                out_ref[a] = value

            return put

        return [(MERGE_AT + MERGE_EVERY * a, MERGE_GAP, merge(parts(a), store(a), w)) for a in range(4)]

    @pl.when(step == 0)
    def _():
        drive(fronts())

    @pl.when((step > 0) & (step < total))
    def _():
        drive(backs() + fronts() + merges())

    @pl.when(step == total)
    def _():
        drive(backs() + merges())


def whole(shape, space=pltpu.VMEM):
    return pl.BlockSpec(shape, lambda i: (0,) * len(shape), memory_space=space)


def interior(tokens, ids, rel_index, bias_table, weights, first, total, before=None, after=None):
    groups = pl.cdiv(SIDE // WIN - 1, GROUP)
    strip = (pl.Element(WIN), pl.Element(SIDE), pl.Element(C))
    extra = () if before is None else (before, after)
    args = (tokens, tokens, ids, rel_index, bias_table, *weights, *extra)
    return pl.pallas_call(
        functools.partial(interior_kernel, first, total),
        grid=(total + 1,),
        out_shape=jax.ShapeDtypeStruct((OUT, OUT, 2 * C), BF16),
        in_specs=[
            pl.BlockSpec(strip, lambda i: (WIN * (first + jnp.minimum(i, total - 1)) + 4, 0, 0)),
            pl.BlockSpec(strip, lambda i: (WIN * (first + jnp.maximum(i - 1, 0)) + 4, 0, 0)),
            whole((STRIPS, SIDE), pltpu.SMEM),
            whole(rel_index.shape),
            whole(bias_table.shape),
        ]
        + [whole(a.shape) for a in weights]
        + [pl.BlockSpec(memory_space=pl.ANY) for _ in extra],
        out_specs=pl.BlockSpec(
            (pl.Element(4), pl.Element(OUT), pl.Element(2 * C)),
            lambda i: (4 * (first + jnp.maximum(i - 1, 0)) + 2, 0, 0),
        ),
        input_output_aliases={} if before is None else {len(args) - 2: 0},
        scratch_shapes=[
            pltpu.VMEM((VARIANTS, SPOTS, HEADS * SPOTS), F32),
            pltpu.VMEM((C, C), BF16),
            pltpu.VMEM((C, MLP), BF16),
            pltpu.VMEM((256, 128), F32),
            pltpu.VMEM((groups, C, SPOTS * GROUP), BF16),
            pltpu.VMEM((WIN, SIDE, C), F32),
            pltpu.VMEM((16 * SPOTS, C), BF16),
            pltpu.VMEM((16 * SPOTS, C), BF16),
            pltpu.VMEM((16 * SPOTS, C), BF16),
            pltpu.VMEM((C, 16 * SPOTS), BF16),
            pltpu.VMEM((16 * SPOTS, C), F32),
            pltpu.VMEM((16 * SPOTS, C), BF16),
            pltpu.VMEM((16 * SPOTS, MLP), BF16),
        ],
        compiler_params=pltpu.CompilerParams(vmem_limit_bytes=18 * 1024 * 1024),
    )(*args)


LINE = 4 * SIDE
BAND = 4 * (SIDE + 8)


def row_specs():
    return [
        pl.BlockSpec((4, SIDE, C), lambda i: (0, 0, 0)),
        pl.BlockSpec((4, SIDE, C), lambda i: (SIDE // 4 - 1, 0, 0)),
    ]


def col_specs():
    return [
        pl.BlockSpec((SIDE, 8, C), lambda i: (0, 0, 0)),
        pl.BlockSpec((SIDE, 8, C), lambda i: (0, SIDE // 8 - 1, 0)),
    ]


def pack_rows_kernel(top_ref, bottom_ref, regions_ref, ids_ref, *messages):
    ids = regions_ref[pl.ds(0, STRIPS, stride=16), :]
    ids_ref[...] = ids
    coded = jnp.concatenate([ids, ids], axis=0).astype(F32).astype(BF16)
    for out, source in zip(messages, (top_ref, bottom_ref)):
        for y in range(4):
            out[pl.ds(SIDE * y, SIDE), :] = source[y].astype(BF16)
        out[pl.ds(LINE, IDROWS), :] = coded


def pack_rows(tokens, regions):
    line = jax.ShapeDtypeStruct((LINE + IDROWS, C), BF16)
    shapes = [jax.ShapeDtypeStruct((STRIPS, SIDE), jnp.int32), line, line]
    return pl.pallas_call(
        pack_rows_kernel,
        grid=(1,),
        out_shape=shapes,
        in_specs=row_specs() + [whole((SIDE, SIDE))],
        out_specs=[whole(a.shape) for a in shapes],
        compiler_params=pltpu.CompilerParams(vmem_limit_bytes=16 * 1024 * 1024),
    )(tokens, tokens, regions)


def pack_cols_kernel(
    left_ref, right_ref, above_any, below_any, ids_ref, after_ref, to_left, to_right, token_ref, band_scr, row_scr,
    above_ref, below_ref, sems,
):
    copies = [
        pltpu.make_async_copy(above_any, above_ref, sems.at[0]),
        pltpu.make_async_copy(below_any, below_ref, sems.at[1]),
    ]
    for copy in copies:
        copy.start()
    for copy in copies:
        copy.wait()
    token_ref[...] = jnp.zeros_like(token_ref)
    row_scr[0] = above_ref[pl.ds(0, LINE), :].astype(F32)
    row_scr[1] = below_ref[pl.ds(0, LINE), :].astype(F32)
    ids = ids_ref[...]
    own = jnp.concatenate([ids, ids], axis=0).astype(F32).astype(BF16)
    for out, source, at, far in ((to_left, left_ref, 0, 0), (to_right, right_ref, 4, SIDE - 4)):
        for y in range(4):
            band_scr[pl.ds(4 * y, 4), :] = row_scr[0, pl.ds(SIDE * y + far, 4), :]
            band_scr[pl.ds(4 * (SIDE + 4 + y), 4), :] = row_scr[1, pl.ds(SIDE * y + far, 4), :]
        for r in range(SIDE):
            band_scr[pl.ds(4 * (r + 4), 4), :] = source[r, pl.ds(at, 4), :]
        out[pl.ds(0, BAND), :] = band_scr[...].astype(BF16)
        out[pl.ds(BAND, IDROWS), :] = above_ref[pl.ds(LINE, IDROWS), :]
        out[pl.ds(BAND + IDROWS, IDROWS), :] = own
        out[pl.ds(BAND + 2 * IDROWS, IDROWS), :] = below_ref[pl.ds(LINE, IDROWS), :]


def pack_cols(tokens, above, below, ids, after):
    band = jax.ShapeDtypeStruct((BAND + 3 * IDROWS, C), BF16)
    token = jax.ShapeDtypeStruct((8, C), F32)
    return pl.pallas_call(
        pack_cols_kernel,
        grid=(1,),
        out_shape=[band, band, token],
        in_specs=col_specs()
        + [pl.BlockSpec(memory_space=pl.ANY)] * 2
        + [whole(ids.shape), pl.BlockSpec(memory_space=pl.ANY)],
        out_specs=[whole(band.shape), whole(band.shape), whole(token.shape)],
        scratch_shapes=[
            pltpu.VMEM((BAND, C), F32),
            pltpu.VMEM((2, LINE, C), F32),
            pltpu.VMEM(above.shape, BF16),
            pltpu.VMEM(below.shape, BF16),
            pltpu.SemaphoreType.DMA((2,)),
        ],
        compiler_params=pltpu.CompilerParams(vmem_limit_bytes=16 * 1024 * 1024),
    )(tokens, tokens, above, below, ids, after)


def moved(value, axis, by):
    size = lax.axis_size(axis)
    return lax.ppermute(value, axis, [(i, (i + by) % size) for i in range(size)])


def gather_border(edges, got, x_scr, msg_scr):
    top, bottom, left, right = edges
    line = 4 * SIDE
    for n in range(2):
        msg_scr[pl.ds(line * n, line), :] = got[n][pl.ds(0, line), :].astype(F32)
        msg_scr[pl.ds(2 * line + BAND * n, BAND), :] = got[2 + n][pl.ds(0, BAND), :].astype(F32)

    def row_of(n):
        return lambda y, at, size: msg_scr[pl.ds(line * n + SIDE * y + at, size), :]

    def col_of(n):
        return lambda r, at, size: msg_scr[pl.ds(2 * line + BAND * n + 4 * (r + 4) + at, size), :]

    def own(ref):
        return lambda y, at, size: ref[y, pl.ds(at, size), :]

    above, below, from_left, from_right = row_of(0), row_of(1), col_of(0), col_of(1)
    for t in range(16):
        for y in range(8):
            turned, spot = WIN * ((y + 4) % 8), WIN * y
            first, second = 4 * y, 32 + 4 * y
            side, at = (above, y) if y < 4 else (own(top), y - 4)
            if t == 0:
                edge = from_left(y - 4, 0, 4)
                x_scr[0, t, pl.ds(turned, 4), :] = edge
                x_scr[0, t, pl.ds(turned + 4, 4), :] = side(at, 0, 4)
            else:
                x_scr[0, t, pl.ds(turned, 8), :] = side(at, 8 * t - 4, 8)
            side, at = (own(bottom), y) if y < 4 else (below, y - 4)
            if t == 15:
                edge = from_right(124 + y, 0, 4)
                x_scr[2, t, pl.ds(spot, 4), :] = side(at, 124, 4)
                x_scr[2, t, pl.ds(spot + 4, 4), :] = edge
            else:
                x_scr[2, t, pl.ds(spot, 8), :] = side(at, 8 * t + 4, 8)
            r = 8 * t - 4 + y
            x_scr[1, t, pl.ds(first, 4), :] = above(y, 124, 4) if r < 0 else own(right)(r, 4, 4)
            x_scr[1, t, pl.ds(second, 4), :] = from_right(r, 0, 4)
            r = 8 * t + 4 + y
            x_scr[3, t, pl.ds(second, 4), :] = from_left(r, 0, 4)
            x_scr[3, t, pl.ds(first, 4), :] = below(r - SIDE, 0, 4) if r >= SIDE else own(left)(r, 0, 4)


def border_patterns(id_at, var_smem):
    for t in range(16):
        before = ((t + 1) // 2 - 1, t // 2)
        after = (t // 2, (t + 1) // 2)
        pairs = (((-1, 0), before), (before, (7, 8)), ((7, 8), after), (after, (-1, 0)))
        for s, (rs, cs) in enumerate(pairs):
            var_smem[s, t] = pattern(id_at(rs[0], cs[0]), id_at(rs[0], cs[1]), id_at(rs[1], cs[0]), id_at(rs[1], cs[1]))


def border_kernel(*refs):
    edges, own_ids, got_any = refs[:4], refs[4], refs[5:9]
    rel_ref, table_ref = refs[9:11]
    w = dict(zip(NAMES, refs[11:19]))
    inner_ref, out_ref = refs[19:21]
    (bias_scr, wvt_scr, wup_scr, pad_scr, att_scr, blk_scr, x_scr, msg_scr, idv_scr, ids_smem, var_smem, row_scr,
     col_scr, row_out, col_out, sem_ids, sem_in, sem_out, got_a, got_b, got_c, got_d, sem_got, nrm_scr, q_scr, k_scr, vt_scr, mid_scr, sec_scr, wide_scr, turn_scr) = refs[21:]
    step = pl.program_id(0)
    count = 16
    col_in = [
        pltpu.make_async_copy(inner_ref.at[:, pl.ds(at, 16), :], col_out.at[n], sem_in.at[n])
        for n, at in enumerate((0, OUT - 16))
    ]

    @pl.when(step == 0)
    def _():
        got = (got_a, got_b, got_c, got_d)
        arrive = [pltpu.make_async_copy(got_any[n], got[n], sem_got.at[n]) for n in range(4)]
        for copy in arrive + col_in:
            copy.start()
        prepare_border(
            rel_ref, table_ref, w["w_qkv"], w["w_up"], bias_scr, wvt_scr, wup_scr, pad_scr, turn_scr
        )
        for copy in arrive:
            copy.wait()
        places = [(0, LINE), (1, LINE)]
        places += [(2 + side, BAND + IDROWS * m) for side in range(2) for m in range(3)]
        for n, (source, first) in enumerate(places):
            idv_scr[pl.ds(STRIPS * n, STRIPS), :] = (
                got[source][pl.ds(first, IDROWS), :].astype(F32)[:STRIPS].astype(jnp.int32)
            )
        ids_copy = pltpu.make_async_copy(idv_scr, ids_smem, sem_ids)
        ids_copy.start()
        gather_border(edges, got, x_scr, msg_scr)
        ids_copy.wait()
        places = {(-1, 0): 0, (1, 0): 1, (-1, -1): 2, (0, -1): 3, (1, -1): 4, (-1, 1): 5, (0, 1): 6, (1, 1): 7}

        def id_at(m, n):
            where = (-1 if m < 0 else int(m >= STRIPS), -1 if n < 0 else int(n >= STRIPS))
            m, n = m % STRIPS, n % STRIPS
            if where == (0, 0):
                return own_ids[m, 16 * n]
            return ids_smem[STRIPS * places[where] + m, 16 * n]

        border_patterns(id_at, var_smem)

    groups = [list(range(at, at + GROUP)) for at in range(0, count, GROUP)]

    def store_att(g):
        def store(i, value):
            att_scr[g, :, pl.ds(32 * i, 32)] = value

        return store

    def store_block(t):
        def store(value):
            blk_scr[pl.ds(32 * t, 32), :] = value

        return store

    def fronts():
        return [
            (
                BORDER_FRONT_EVERY * g,
                FRONT_GAP,
                front(
                    [lambda t=t: x_scr[step, t] for t in ts],
                    store_att(g),
                    [VARIANTS * step + var_smem[step, t] for t in ts],
                    w,
                    bias_scr,
                    wvt_scr,
                    SPOTS * ts[0],
                    nrm_scr, q_scr, k_scr,
                    vt_scr,
                    nq=32,
                ),
            )
            for g, ts in enumerate(groups)
        ]

    def backs():
        return [
            (
                BORDER_BACK_EVERY * g,
                BACK_GAP,
                back(
                    [lambda t=t: x_scr[step - 1, t, pl.ds(0, 32), :] for t in ts],
                    lambda g=g: att_scr[g],
                    [store_block(t) for t in ts],
                    w,
                    wup_scr,
                    32 * ts[0],
                    mid_scr,
                    sec_scr,
                    wide_scr,
                    nq=32,
                ),
            )
            for g, ts in enumerate(groups)
        ]

    @pl.when(step == 0)
    def _():
        drive(fronts())

    @pl.when((step > 0) & (step < 4))
    def _():
        drive(backs() + fronts())

    @pl.when(step == 4)
    def _():
        drive(backs())

    def spread(scr, at, first, value):
        for half in range(2):
            scr[2 * at + half, pl.ds(first, count, stride=4), :] = value[:, C * half : C * (half + 1)]

    def both(scr, at, rows):
        return jnp.concatenate([scr[2 * at + half, rows, :] for half in range(2)], axis=1)

    def merged(spots):
        joined = [
            jnp.concatenate([blk_scr[pl.ds(four[n], count, stride=32), :] for four in spots], axis=0)
            for n in range(4)
        ]
        normed = layer_norm(jnp.concatenate(joined, axis=1), w["gm"][...]).astype(BF16)
        out = jnp.dot(normed, w["w_merge"][...], preferred_element_type=F32)
        return [out[count * n : count * (n + 1)] for n in range(len(spots))]

    def row_merged():
        for a in range(2):
            fours = [[(2 * a + dy) * WIN + 2 * b + dx for dx in range(2) for dy in range(2)] for b in range(4)]
            for b, value in enumerate(merged(fours)):
                yield a, b, value

    def col_merged():
        for b in range(2):
            fours = [[(2 * a + dy) * 4 + 2 * b + dx for dx in range(2) for dy in range(2)] for a in range(4)]
            for a, value in enumerate(merged(fours)):
                yield a, b, value

    @pl.when(step == 1)
    def _():
        for a, b, value in row_merged():
            spread(row_scr, a, 8 + b - 2, value)

    @pl.when(step == 2)
    def _():
        for a, b, value in col_merged():
            spread(col_scr, 2 + b, 8 + a - 2, value)

    @pl.when(step == 3)
    def _():
        for a, b, value in row_merged():
            spread(row_scr, 2 + a, 8 + b + 2, value)

    @pl.when(step == 4)
    def _():
        for a, b, value in col_merged():
            spread(col_scr, b, 8 + a + 2, value)

    @pl.when(step == 4)
    def _():
        for c in range(2):
            for a in range(2):
                for h in range(2):
                    row_scr[2 * a + h, pl.ds(8 + OUT - 2 + c, 1), :] = col_scr[2 * (2 + c) + h, pl.ds(8 + a, 1), :]
                    row_scr[2 * (2 + a) + h, pl.ds(8 + c, 1), :] = col_scr[2 * c + h, pl.ds(8 + OUT - 2 + a, 1), :]
        for a in range(4):
            row_out[a] = both(row_scr, a, pl.ds(8, OUT)).astype(BF16)
        for copy in col_in:
            copy.wait()
        place = lax.broadcasted_iota(jnp.int32, (16, 2 * C), 0)
        for side, first in ((0, 0), (1, 14)):
            for r in range(2, OUT - 2):
                old = col_out[side, r].astype(F32)
                for c in range(2):
                    old = jnp.where(place == first + c, both(col_scr, 2 * side + c, pl.ds(8 + r, 1)), old)
                col_out[side, r] = old.astype(BF16)
        inside = pl.ds(2, OUT - 4)
        copies = [
            pltpu.make_async_copy(
                col_out.at[n, inside], out_ref.at[inside, pl.ds(at, 16), :], sem_out.at[n]
            )
            for n, at in enumerate((0, OUT - 16))
        ]
        copies += [
            pltpu.make_async_copy(row_out.at[pl.ds(2 * n, 2)], out_ref.at[pl.ds(at, 2)], sem_out.at[2 + n])
            for n, at in enumerate((0, OUT - 2))
        ]
        for copy in copies:
            copy.start()
        for copy in copies:
            copy.wait()


def border(tokens, ids, got, rel_index, bias_table, weights, inner):
    return pl.pallas_call(
        border_kernel,
        grid=(5,),
        out_shape=jax.ShapeDtypeStruct((OUT, OUT, 2 * C), BF16),
        in_specs=row_specs()
        + col_specs()
        + [whole((STRIPS, SIDE), pltpu.SMEM)]
        + [pl.BlockSpec(memory_space=pl.ANY) for _ in got]
        + [whole(rel_index.shape), whole(bias_table.shape)]
        + [whole(a.shape) for a in weights]
        + [pl.BlockSpec(memory_space=pl.ANY)],
        out_specs=pl.BlockSpec(memory_space=pl.ANY),
        input_output_aliases={11 + len(weights): 0},
        scratch_shapes=[
            pltpu.VMEM((4 * VARIANTS, SPOTS, HEADS * 32), F32),
            pltpu.VMEM((C, C), BF16),
            pltpu.VMEM((C, MLP), BF16),
            pltpu.VMEM((256, 128), F32),
            pltpu.VMEM((16 // GROUP, C, 32 * GROUP), BF16),
            pltpu.VMEM((16 * SPOTS, C), F32),
            pltpu.VMEM((4, 16, SPOTS, C), F32),
            pltpu.VMEM((2 * LINE + 2 * BAND, C), F32),
            pltpu.VMEM((8 * STRIPS, SIDE), jnp.int32),
            pltpu.SMEM((8 * STRIPS, SIDE), jnp.int32),
            pltpu.SMEM((4, 16), jnp.int32),
            pltpu.VMEM((8, OUT + 16, C), F32),
            pltpu.VMEM((8, OUT + 16, C), F32),
            pltpu.VMEM((4, OUT, 2 * C), BF16),
            pltpu.VMEM((2, OUT, 16, 2 * C), BF16),
            pltpu.SemaphoreType.DMA,
            pltpu.SemaphoreType.DMA((2,)),
            pltpu.SemaphoreType.DMA((4,)),
            *[pltpu.VMEM(a.shape, BF16) for a in got],
            pltpu.SemaphoreType.DMA((4,)),
            pltpu.VMEM((16 * SPOTS, C), BF16),
            pltpu.VMEM((16 * SPOTS, C), BF16),
            pltpu.VMEM((16 * SPOTS, C), BF16),
            pltpu.VMEM((C, 16 * SPOTS), BF16),
            pltpu.VMEM((16 * SPOTS, C), F32),
            pltpu.VMEM((16 * SPOTS, C), BF16),
            pltpu.VMEM((16 * SPOTS, MLP), BF16),
            pltpu.VMEM((128, 128), F32),
        ],
        compiler_params=pltpu.CompilerParams(vmem_limit_bytes=26 * 1024 * 1024),
    )(tokens, tokens, tokens, tokens, ids, *got, rel_index, bias_table, *weights, inner)


def on_device(
    tokens, regions, rel_index, bias_table, norm1_gain, w_qkv, w_proj, norm2_gain, w_up, w_down, merge_gain, w_merge
):
    weights = (
        norm1_gain.reshape(1, C), w_qkv, w_proj, norm2_gain.reshape(1, C), w_up, w_down,
        merge_gain.reshape(1, 4 * C), w_merge,
    )
    bias_table = bias_table.T
    tokens = pltpu.with_memory_space_constraint(tokens, pltpu.HBM)
    ids, top, bottom = pack_rows(tokens, regions)
    above, below = moved(bottom, "row", 1), moved(top, "row", -1)
    inner = interior(tokens, ids, rel_index, bias_table, weights, 0, EARLY)
    inner = pltpu.with_memory_space_constraint(inner, pltpu.HBM)
    to_left, to_right, token = pack_cols(tokens, above, below, ids, inner)
    from_left, from_right = moved(to_right, "col", 1), moved(to_left, "col", -1)
    inner = interior(
        tokens, ids, rel_index, bias_table, weights, EARLY, SIDE // WIN - 1 - EARLY, before=inner, after=token
    )
    return border(
        tokens, ids, (above, below, from_left, from_right), rel_index, bias_table, weights, inner
    )


def solution(mesh):
    return jax.shard_map(
        on_device,
        mesh=mesh,
        in_specs=(P("row", "col", None), P("row", "col")) + (P(),) * 10,
        out_specs=P("row", "col", None),
        check_vma=False,
    )
```

```python
import functools

import jax
import jax.numpy as jnp
from jax import lax
from jax.experimental import pallas as pl
from jax.experimental.pallas import tpu as pltpu
from jax.sharding import PartitionSpec as P

C = 128
HEADS = 4
HD = 32
WIN = 8
SPOTS = WIN * WIN
MLP = 512
SIDE = 128
OUT = SIDE // 2
STRIPS = SIDE // 16
IDROWS = 16
EARLY = 3
LOG2E = 1.4426950408889634
QSCALE = HD ** (-0.5) * LOG2E
VARIANTS = 24
F32 = jnp.float32
BF16 = jnp.bfloat16
NT = (((1,), (1,)), ((), ()))
TN = (((0,), (0,)), ((), ()))


def layer_norm(values, gain):
    mean = jnp.mean(values, axis=-1, keepdims=True)
    centred = values - mean
    var = jnp.mean(centred * centred, axis=-1, keepdims=True)
    return centred * lax.rsqrt(var + 1e-05) * gain


def half_gelu(half):
    h = half.astype(BF16)
    c0 = jnp.asarray(2.0 * 0.7978845608028654, BF16)
    c1 = jnp.asarray(8.0 * 0.7978845608028654 * 0.044715, BF16)
    inner = h * (c0 + c1 * (h * h))
    return h + h * jnp.tanh(inner)


def prepare_weights(table_ref, w_qkv_ref, w_up_ref, wvt_scr, wup_scr, pad_scr):
    wvt_scr[...] = w_qkv_ref[:, 2 * C :].astype(F32).T.astype(BF16)
    wup_scr[...] = w_up_ref[...] * jnp.asarray(0.5, BF16)
    pad_scr[...] = jnp.zeros_like(pad_scr)
    rest = table_ref.shape[1] - 128
    pad_scr[pl.ds(128, HEADS), :] = table_ref[:, :128]
    pad_scr[pl.ds(136, HEADS), pl.ds(0, rest)] = table_ref[:, 128:]


def from_table(rel, head, pad_scr):
    low = rel < 128
    spot = jnp.where(low, rel, rel - 128)
    got = []
    for first in (128, 136):
        row = jnp.broadcast_to(pad_scr[pl.ds(first + head, 1), :], rel.shape)
        got.append(jnp.take_along_axis(row, spot, axis=1, mode="promise_in_bounds"))
    return jnp.where(low, got[0], got[1]) * LOG2E


def fill_variants(bias_scr, first, bias, key_quarter, query_quarter):
    def label_of(quarter, labels):
        return jnp.where(
            quarter == 0, 0, jnp.where(quarter == 1, labels[0], jnp.where(quarter == 2, labels[1], labels[2]))
        )

    for one in range(2):
        for two in (0, 1, 2) if one else (0, 2):
            for three in range(4):
                if (three == 1 and not one) or (three == 2 and two != 2):
                    continue
                same = label_of(key_quarter, (one, two, three)) == label_of(query_quarter, (one, two, three))
                bias_scr[first + one * 12 + two * 4 + three] = jnp.where(same, bias, -1e30)


def prepare(rel_ref, table_ref, w_qkv_ref, w_up_ref, bias_scr, wvt_scr, wup_scr, pad_scr):
    prepare_weights(table_ref, w_qkv_ref, w_up_ref, wvt_scr, wup_scr, pad_scr)
    pad_scr[pl.ds(0, SPOTS), pl.ds(0, SPOTS)] = rel_ref[...].astype(F32)
    rel_t = pad_scr[pl.ds(0, 128), :].T[:SPOTS, :].astype(jnp.int32)
    lane = lax.broadcasted_iota(jnp.int32, (SPOTS, 128), 1)
    rel_t = jnp.where(lane < SPOTS, rel_t, pltpu.roll(rel_t, SPOTS, 1))
    halves = []
    for pair in range(HEADS // 2):
        per_head = [from_table(rel_t, head, pad_scr) for head in (2 * pair, 2 * pair + 1)]
        halves.append(jnp.where(lane < SPOTS, per_head[0], per_head[1]))

    def quarter(spots):
        return spots // 32 * 2 + spots % WIN // 4

    fill_variants(
        bias_scr,
        0,
        jnp.concatenate(halves, axis=1),
        quarter(lax.broadcasted_iota(jnp.int32, (SPOTS, 1), 0)),
        quarter(lax.broadcasted_iota(jnp.int32, (1, 2 * 128), 1) % SPOTS),
    )


def border_spot(strip, spot):
    if strip in (0, 2):
        return (spot + 32 * (strip == 0)) % SPOTS
    half, y, x = spot // 32, spot % 32 // 4, spot % 4
    return y * WIN + (half if strip == 1 else 1 - half) * 4 + x


def border_quarter(strip, spots):
    half = spots // 32
    if strip == 0:
        return (1 - half) * 2 + spots % WIN // 4
    if strip == 2:
        return half * 2 + spots % WIN // 4
    return spots % 32 // 16 * 2 + (half if strip == 1 else 1 - half)


def prepare_border(rel_ref, table_ref, w_qkv_ref, w_up_ref, bias_scr, wvt_scr, wup_scr, pad_scr, turn_scr):
    prepare_weights(table_ref, w_qkv_ref, w_up_ref, wvt_scr, wup_scr, pad_scr)
    lane = lax.broadcasted_iota(jnp.int32, (SPOTS, 128), 1)
    turn_scr[...] = jnp.zeros_like(turn_scr)
    for strip in range(4):
        for at in range(0, SPOTS, 4):
            pad_scr[pl.ds(at, 4), pl.ds(0, SPOTS)] = rel_ref[pl.ds(border_spot(strip, at), 4), :].astype(F32)
        turn_scr[...] = pad_scr[pl.ds(0, 128), :].T
        rel_t = jnp.concatenate(
            [turn_scr[pl.ds(border_spot(strip, at), 4), :] for at in range(0, SPOTS, 4)], axis=0
        )
        rel_t = jnp.where(lane < 32, rel_t, 0.0)
        rel_t = rel_t + pltpu.roll(rel_t, 32, 1)
        rel_t = (rel_t + pltpu.roll(rel_t, 64, 1)).astype(jnp.int32)
        bias = from_table(rel_t, 0, pad_scr)
        for head in range(1, HEADS):
            bias = jnp.where(lane // 32 == head, from_table(rel_t, head, pad_scr), bias)
        fill_variants(
            bias_scr,
            VARIANTS * strip,
            bias,
            border_quarter(strip, lax.broadcasted_iota(jnp.int32, (SPOTS, 1), 0)),
            border_quarter(strip, lax.broadcasted_iota(jnp.int32, (1, 128), 1) % 32),
        )


def pattern(top_left, top_right, low_left, low_right):
    one = jnp.where(top_right == top_left, 0, 1)
    two = jnp.where(low_left == top_left, 0, jnp.where(low_left == top_right, 1, 2))
    three = jnp.where(
        low_right == top_left,
        0,
        jnp.where(low_right == top_right, 1, jnp.where(low_right == low_left, 2, 3)),
    )
    return one * 12 + two * 4 + three


def front(loads, store_att, variants, w, bias_scr, wvt_scr, base, nrm_scr, q_scr, k_scr, vt_scr, nq=SPOTS):
    for i, load in enumerate(loads):
        nrm_scr[pl.ds(base + SPOTS * i, SPOTS), :] = layer_norm(load(), w["g1"][...]).astype(BF16)
        yield
    size = SPOTS * len(loads)
    for at in range(0, size, QPIECE):
        piece = min(QPIECE, size - at)
        rows = pl.ds(base + at, piece)
        qk = jnp.dot(nrm_scr[rows, :], w["w_qkv"][:, : 2 * C], preferred_element_type=F32)
        for i in range(0, piece, SPOTS):
            part = qk[i : i + SPOTS]
            q_scr[pl.ds(base + at + i, SPOTS), :] = (part[:, :C] * QSCALE).astype(BF16)
            k_scr[pl.ds(base + at + i, SPOTS), :] = part[:, C:].astype(BF16)
        yield
    for at in range(0, size, 256):
        wide = min(256, size - at)
        vt_scr[:, pl.ds(base + at, wide)] = lax.dot_general(
            wvt_scr[...], nrm_scr[pl.ds(base + at, wide), :], NT, preferred_element_type=F32
        ).astype(BF16)
    yield
    lane = lax.broadcasted_iota(jnp.int32, (1, C), 1)
    n = len(loads)
    st, ot = {}, {}
    for i in range(n + 2 * LAG):
        if i < n:
            rows = pl.ds(base + SPOTS * i, SPOTS)
            q = q_scr[pl.ds(base + SPOTS * i, nq), :]
            k = k_scr[rows, :]
            qm = jnp.concatenate([jnp.where(lane // HD == h, q, jnp.zeros_like(q)) for h in range(HEADS)], axis=0)
            st[i] = lax.dot_general(k, qm, NT, preferred_element_type=F32)
        at = i - LAG
        if 0 <= at < n:
            rows = slice(SPOTS * at, SPOTS * (at + 1))
            scores = st.pop(at) + bias_scr[variants[at]]
            top = jnp.max(scores, axis=0, keepdims=True)
            p = jnp.exp2((scores - top).astype(BF16))
            vw = jnp.concatenate([vt_scr[:, pl.ds(base + SPOTS * at, SPOTS)], jnp.ones((16, SPOTS), BF16)], axis=0)
            ot[at] = jnp.dot(vw, p, preferred_element_type=F32)
        at = i - 2 * LAG
        if 0 <= at < n:
            got = ot.pop(at)
            inv = 1.0 / got[C : C + 1]
            store_att(
                at,
                jnp.concatenate(
                    [
                        got[HD * h : HD * (h + 1), nq * h : nq * (h + 1)]
                        * inv[:, nq * h : nq * (h + 1)]
                        for h in range(HEADS)
                    ],
                    axis=0,
                ).astype(BF16),
            )
        yield


def back(loads, load_att, stores, w, wup_scr, base, mid_scr, sec_scr, wide_scr, nq=SPOTS):
    size = nq * len(loads)
    proj = lax.dot_general(load_att(), w["w_proj"][...], TN, preferred_element_type=F32)
    yield
    for i, load in enumerate(loads):
        rows = pl.ds(base + nq * i, nq)
        mid = load() + proj[nq * i : nq * (i + 1)]
        mid_scr[rows, :] = mid
        sec_scr[rows, :] = layer_norm(mid, w["g2"][...]).astype(BF16)
        yield
    for at in range(0, size, PIECE):
        piece = min(PIECE, size - at)
        up = jnp.dot(sec_scr[pl.ds(base + at, piece), :], wup_scr[...], preferred_element_type=F32)
        yield
        for i in range(0, piece, 32):
            wide_scr[pl.ds(base + at + i, 32), :] = half_gelu(up[i : i + 32])
            if i % 64:
                yield
    down = jnp.dot(wide_scr[pl.ds(base, size), :], w["w_down"][...], preferred_element_type=F32)
    yield
    for i, store in enumerate(stores):
        store(mid_scr[pl.ds(base + nq * i, nq), :] + down[nq * i : nq * (i + 1)])
        yield


PIECE = 256
QPIECE = 256
LAG = 2


def merge(load_parts, store, w):
    joined = jnp.concatenate(load_parts(), axis=1)
    normed = layer_norm(joined, w["gm"][...]).astype(BF16)
    yield
    out = jnp.dot(normed, w["w_merge"][...], preferred_element_type=F32)
    yield
    store(out.astype(BF16))


def drive(timed):
    events = []
    for number, (start, gap, gen) in enumerate(timed):
        for step in range(80):
            events.append((start + gap * step, number, gen))
    for _, _, gen in sorted(events, key=lambda e: (e[0], e[1])):
        next(gen, None)


NAMES = ("g1", "w_qkv", "w_proj", "g2", "w_up", "w_down", "gm", "w_merge")
GROUP = 8
FRONT_AT = 0
FRONT_EVERY, FRONT_GAP = 20, 1
BACK_EVERY, BACK_GAP = 16, 0.8
BORDER_FRONT_EVERY, BORDER_BACK_EVERY = 10, 12
MERGE_EVERY, MERGE_GAP, MERGE_AT = 1.0, 1.0, 50


def interior_kernel(first, total, x_ref, old_ref, ids_ref, rel_ref, table_ref, *refs):
    w = dict(zip(NAMES, refs[:8]))
    out_ref = refs[-14]
    (bias_scr, wvt_scr, wup_scr, pad_scr, att_scr, blk_scr, nrm_scr, q_scr, k_scr, vt_scr, mid_scr, sec_scr, wide_scr) = refs[-13:]
    step = pl.program_id(0)
    count = SIDE // WIN - 1

    @pl.when(step == 0)
    def _():
        prepare(rel_ref, table_ref, w["w_qkv"], w["w_up"], bias_scr, wvt_scr, wup_scr, pad_scr)
        blk_scr[...] = jnp.zeros_like(blk_scr)

    upper = jnp.minimum(first + step, count - 1) // 2
    lower = jnp.minimum(first + step + 1, count) // 2

    def loader(ref, j):
        return lambda: jnp.concatenate([ref[y, pl.ds(WIN * j + 4, WIN), :] for y in range(WIN)], axis=0)

    def variant(j):
        left, right = 16 * (j // 2), 16 * ((j + 1) // 2)
        return pattern(ids_ref[upper, left], ids_ref[upper, right], ids_ref[lower, left], ids_ref[lower, right])

    def store_att(g):
        def store(i, value):
            att_scr[g, :, pl.ds(SPOTS * i, SPOTS)] = value

        return store

    def store_block(j):
        def store(value):
            for y in range(WIN):
                blk_scr[y, pl.ds(WIN * j + 4, WIN), :] = value[WIN * y : WIN * (y + 1)]

        return store

    groups = [list(range(at, min(at + GROUP, count))) for at in range(0, count, GROUP)]

    def fronts():
        return [
            (
                FRONT_AT + FRONT_EVERY * g,
                FRONT_GAP,
                front([loader(x_ref, j) for j in js], store_att(g), [variant(j) for j in js], w, bias_scr, wvt_scr, SPOTS * js[0], nrm_scr, q_scr, k_scr, vt_scr),
            )
            for g, js in enumerate(groups)
        ]

    def backs():
        return [
            (
                BACK_EVERY * g,
                BACK_GAP,
                back(
                    [loader(old_ref, j) for j in js],
                    lambda g=g, js=js: att_scr[g, :, : SPOTS * len(js)],
                    [store_block(j) for j in js],
                    w,
                    wup_scr,
                    SPOTS * js[0],
                    mid_scr,
                    sec_scr,
                    wide_scr,
                ),
            )
            for g, js in enumerate(groups)
        ]

    def merges():
        def parts(a):
            return lambda: [blk_scr[2 * a + dy, pl.ds(dx, OUT, stride=2), :] for dx in range(2) for dy in range(2)]

        def store(a):
            def put(value):
                out_ref[a] = value

            return put

        return [(MERGE_AT + MERGE_EVERY * a, MERGE_GAP, merge(parts(a), store(a), w)) for a in range(4)]

    @pl.when(step == 0)
    def _():
        drive(fronts())

    @pl.when((step > 0) & (step < total))
    def _():
        drive(backs() + fronts() + merges())

    @pl.when(step == total)
    def _():
        drive(backs() + merges())


def whole(shape, space=pltpu.VMEM):
    return pl.BlockSpec(shape, lambda i: (0,) * len(shape), memory_space=space)


def interior(tokens, ids, rel_index, bias_table, weights, first, total, before=None, after=None):
    groups = pl.cdiv(SIDE // WIN - 1, GROUP)
    strip = (pl.Element(WIN), pl.Element(SIDE), pl.Element(C))
    extra = () if before is None else (before, after)
    args = (tokens, tokens, ids, rel_index, bias_table, *weights, *extra)
    return pl.pallas_call(
        functools.partial(interior_kernel, first, total),
        grid=(total + 1,),
        out_shape=jax.ShapeDtypeStruct((OUT, OUT, 2 * C), BF16),
        in_specs=[
            pl.BlockSpec(strip, lambda i: (WIN * (first + jnp.minimum(i, total - 1)) + 4, 0, 0)),
            pl.BlockSpec(strip, lambda i: (WIN * (first + jnp.maximum(i - 1, 0)) + 4, 0, 0)),
            whole((STRIPS, SIDE), pltpu.SMEM),
            whole(rel_index.shape),
            whole(bias_table.shape),
        ]
        + [whole(a.shape) for a in weights]
        + [pl.BlockSpec(memory_space=pl.ANY) for _ in extra],
        out_specs=pl.BlockSpec(
            (pl.Element(4), pl.Element(OUT), pl.Element(2 * C)),
            lambda i: (4 * (first + jnp.maximum(i - 1, 0)) + 2, 0, 0),
        ),
        input_output_aliases={} if before is None else {len(args) - 2: 0},
        scratch_shapes=[
            pltpu.VMEM((VARIANTS, SPOTS, HEADS * SPOTS), F32),
            pltpu.VMEM((C, C), BF16),
            pltpu.VMEM((C, MLP), BF16),
            pltpu.VMEM((256, 128), F32),
            pltpu.VMEM((groups, C, SPOTS * GROUP), BF16),
            pltpu.VMEM((WIN, SIDE, C), F32),
            pltpu.VMEM((16 * SPOTS, C), BF16),
            pltpu.VMEM((16 * SPOTS, C), BF16),
            pltpu.VMEM((16 * SPOTS, C), BF16),
            pltpu.VMEM((C, 16 * SPOTS), BF16),
            pltpu.VMEM((16 * SPOTS, C), F32),
            pltpu.VMEM((16 * SPOTS, C), BF16),
            pltpu.VMEM((16 * SPOTS, MLP), BF16),
        ],
        compiler_params=pltpu.CompilerParams(vmem_limit_bytes=18 * 1024 * 1024),
    )(*args)


LINE = 4 * SIDE
BAND = 4 * (SIDE + 8)


def row_specs():
    return [
        pl.BlockSpec((4, SIDE, C), lambda i: (0, 0, 0)),
        pl.BlockSpec((4, SIDE, C), lambda i: (SIDE // 4 - 1, 0, 0)),
    ]


def col_specs():
    return [
        pl.BlockSpec((SIDE, 8, C), lambda i: (0, 0, 0)),
        pl.BlockSpec((SIDE, 8, C), lambda i: (0, SIDE // 8 - 1, 0)),
    ]


def pack_rows_kernel(top_ref, bottom_ref, regions_ref, ids_ref, *messages):
    ids = regions_ref[pl.ds(0, STRIPS, stride=16), :]
    ids_ref[...] = ids
    coded = jnp.concatenate([ids, ids], axis=0).astype(F32).astype(BF16)
    for out, source in zip(messages, (top_ref, bottom_ref)):
        for y in range(4):
            out[pl.ds(SIDE * y, SIDE), :] = source[y].astype(BF16)
        out[pl.ds(LINE, IDROWS), :] = coded


def pack_rows(tokens, regions):
    line = jax.ShapeDtypeStruct((LINE + IDROWS, C), BF16)
    shapes = [jax.ShapeDtypeStruct((STRIPS, SIDE), jnp.int32), line, line]
    return pl.pallas_call(
        pack_rows_kernel,
        grid=(1,),
        out_shape=shapes,
        in_specs=row_specs() + [whole((SIDE, SIDE))],
        out_specs=[whole(a.shape) for a in shapes],
        compiler_params=pltpu.CompilerParams(vmem_limit_bytes=16 * 1024 * 1024),
    )(tokens, tokens, regions)


def pack_cols_kernel(
    left_ref, right_ref, above_any, below_any, ids_ref, after_ref, to_left, to_right, token_ref, band_scr, row_scr,
    above_ref, below_ref, sems,
):
    copies = [
        pltpu.make_async_copy(above_any, above_ref, sems.at[0]),
        pltpu.make_async_copy(below_any, below_ref, sems.at[1]),
    ]
    for copy in copies:
        copy.start()
    for copy in copies:
        copy.wait()
    token_ref[...] = jnp.zeros_like(token_ref)
    row_scr[0] = above_ref[pl.ds(0, LINE), :].astype(F32)
    row_scr[1] = below_ref[pl.ds(0, LINE), :].astype(F32)
    ids = ids_ref[...]
    own = jnp.concatenate([ids, ids], axis=0).astype(F32).astype(BF16)
    for out, source, at, far in ((to_left, left_ref, 0, 0), (to_right, right_ref, 4, SIDE - 4)):
        for y in range(4):
            band_scr[pl.ds(4 * y, 4), :] = row_scr[0, pl.ds(SIDE * y + far, 4), :]
            band_scr[pl.ds(4 * (SIDE + 4 + y), 4), :] = row_scr[1, pl.ds(SIDE * y + far, 4), :]
        for r in range(SIDE):
            band_scr[pl.ds(4 * (r + 4), 4), :] = source[r, pl.ds(at, 4), :]
        out[pl.ds(0, BAND), :] = band_scr[...].astype(BF16)
        out[pl.ds(BAND, IDROWS), :] = above_ref[pl.ds(LINE, IDROWS), :]
        out[pl.ds(BAND + IDROWS, IDROWS), :] = own
        out[pl.ds(BAND + 2 * IDROWS, IDROWS), :] = below_ref[pl.ds(LINE, IDROWS), :]


def pack_cols(tokens, above, below, ids, after):
    band = jax.ShapeDtypeStruct((BAND + 3 * IDROWS, C), BF16)
    token = jax.ShapeDtypeStruct((8, C), F32)
    return pl.pallas_call(
        pack_cols_kernel,
        grid=(1,),
        out_shape=[band, band, token],
        in_specs=col_specs()
        + [pl.BlockSpec(memory_space=pl.ANY)] * 2
        + [whole(ids.shape), pl.BlockSpec(memory_space=pl.ANY)],
        out_specs=[whole(band.shape), whole(band.shape), whole(token.shape)],
        scratch_shapes=[
            pltpu.VMEM((BAND, C), F32),
            pltpu.VMEM((2, LINE, C), F32),
            pltpu.VMEM(above.shape, BF16),
            pltpu.VMEM(below.shape, BF16),
            pltpu.SemaphoreType.DMA((2,)),
        ],
        compiler_params=pltpu.CompilerParams(vmem_limit_bytes=16 * 1024 * 1024),
    )(tokens, tokens, above, below, ids, after)


def moved(value, axis, by):
    size = lax.axis_size(axis)
    return lax.ppermute(value, axis, [(i, (i + by) % size) for i in range(size)])


def gather_border(edges, got, x_scr, msg_scr):
    top, bottom, left, right = edges
    line = 4 * SIDE
    for n in range(2):
        msg_scr[pl.ds(line * n, line), :] = got[n][pl.ds(0, line), :].astype(F32)
        msg_scr[pl.ds(2 * line + BAND * n, BAND), :] = got[2 + n][pl.ds(0, BAND), :].astype(F32)

    def row_of(n):
        return lambda y, at, size: msg_scr[pl.ds(line * n + SIDE * y + at, size), :]

    def col_of(n):
        return lambda r, at, size: msg_scr[pl.ds(2 * line + BAND * n + 4 * (r + 4) + at, size), :]

    def own(ref):
        return lambda y, at, size: ref[y, pl.ds(at, size), :]

    above, below, from_left, from_right = row_of(0), row_of(1), col_of(0), col_of(1)
    for t in range(16):
        for y in range(8):
            turned, spot = WIN * ((y + 4) % 8), WIN * y
            first, second = 4 * y, 32 + 4 * y
            side, at = (above, y) if y < 4 else (own(top), y - 4)
            if t == 0:
                edge = from_left(y - 4, 0, 4)
                x_scr[0, t, pl.ds(turned, 4), :] = edge
                x_scr[0, t, pl.ds(turned + 4, 4), :] = side(at, 0, 4)
            else:
                x_scr[0, t, pl.ds(turned, 8), :] = side(at, 8 * t - 4, 8)
            side, at = (own(bottom), y) if y < 4 else (below, y - 4)
            if t == 15:
                edge = from_right(124 + y, 0, 4)
                x_scr[2, t, pl.ds(spot, 4), :] = side(at, 124, 4)
                x_scr[2, t, pl.ds(spot + 4, 4), :] = edge
            else:
                x_scr[2, t, pl.ds(spot, 8), :] = side(at, 8 * t + 4, 8)
            r = 8 * t - 4 + y
            x_scr[1, t, pl.ds(first, 4), :] = above(y, 124, 4) if r < 0 else own(right)(r, 4, 4)
            x_scr[1, t, pl.ds(second, 4), :] = from_right(r, 0, 4)
            r = 8 * t + 4 + y
            x_scr[3, t, pl.ds(second, 4), :] = from_left(r, 0, 4)
            x_scr[3, t, pl.ds(first, 4), :] = below(r - SIDE, 0, 4) if r >= SIDE else own(left)(r, 0, 4)


def border_patterns(id_at, var_smem):
    for t in range(16):
        before = ((t + 1) // 2 - 1, t // 2)
        after = (t // 2, (t + 1) // 2)
        pairs = (((-1, 0), before), (before, (7, 8)), ((7, 8), after), (after, (-1, 0)))
        for s, (rs, cs) in enumerate(pairs):
            var_smem[s, t] = pattern(id_at(rs[0], cs[0]), id_at(rs[0], cs[1]), id_at(rs[1], cs[0]), id_at(rs[1], cs[1]))


def border_kernel(*refs):
    edges, own_ids, got_any = refs[:4], refs[4], refs[5:9]
    rel_ref, table_ref = refs[9:11]
    w = dict(zip(NAMES, refs[11:19]))
    inner_ref, out_ref = refs[19:21]
    (bias_scr, wvt_scr, wup_scr, pad_scr, att_scr, blk_scr, x_scr, msg_scr, idv_scr, ids_smem, var_smem, row_scr,
     col_scr, row_out, col_out, sem_ids, sem_in, sem_out, got_a, got_b, got_c, got_d, sem_got, nrm_scr, q_scr, k_scr, vt_scr, mid_scr, sec_scr, wide_scr, turn_scr) = refs[21:]
    step = pl.program_id(0)
    count = 16
    col_in = [
        pltpu.make_async_copy(inner_ref.at[:, pl.ds(at, 16), :], col_out.at[n], sem_in.at[n])
        for n, at in enumerate((0, OUT - 16))
    ]

    @pl.when(step == 0)
    def _():
        got = (got_a, got_b, got_c, got_d)
        arrive = [pltpu.make_async_copy(got_any[n], got[n], sem_got.at[n]) for n in range(4)]
        for copy in arrive + col_in:
            copy.start()
        prepare_border(
            rel_ref, table_ref, w["w_qkv"], w["w_up"], bias_scr, wvt_scr, wup_scr, pad_scr, turn_scr
        )
        for copy in arrive:
            copy.wait()
        places = [(0, LINE), (1, LINE)]
        places += [(2 + side, BAND + IDROWS * m) for side in range(2) for m in range(3)]
        for n, (source, first) in enumerate(places):
            idv_scr[pl.ds(STRIPS * n, STRIPS), :] = (
                got[source][pl.ds(first, IDROWS), :].astype(F32)[:STRIPS].astype(jnp.int32)
            )
        ids_copy = pltpu.make_async_copy(idv_scr, ids_smem, sem_ids)
        ids_copy.start()
        gather_border(edges, got, x_scr, msg_scr)
        ids_copy.wait()
        places = {(-1, 0): 0, (1, 0): 1, (-1, -1): 2, (0, -1): 3, (1, -1): 4, (-1, 1): 5, (0, 1): 6, (1, 1): 7}

        def id_at(m, n):
            where = (-1 if m < 0 else int(m >= STRIPS), -1 if n < 0 else int(n >= STRIPS))
            m, n = m % STRIPS, n % STRIPS
            if where == (0, 0):
                return own_ids[m, 16 * n]
            return ids_smem[STRIPS * places[where] + m, 16 * n]

        border_patterns(id_at, var_smem)

    groups = [list(range(at, at + GROUP)) for at in range(0, count, GROUP)]

    def store_att(g):
        def store(i, value):
            att_scr[g, :, pl.ds(32 * i, 32)] = value

        return store

    def store_block(t):
        def store(value):
            blk_scr[pl.ds(32 * t, 32), :] = value

        return store

    def fronts():
        return [
            (
                BORDER_FRONT_EVERY * g,
                FRONT_GAP,
                front(
                    [lambda t=t: x_scr[step, t] for t in ts],
                    store_att(g),
                    [VARIANTS * step + var_smem[step, t] for t in ts],
                    w,
                    bias_scr,
                    wvt_scr,
                    SPOTS * ts[0],
                    nrm_scr, q_scr, k_scr,
                    vt_scr,
                    nq=32,
                ),
            )
            for g, ts in enumerate(groups)
        ]

    def backs():
        return [
            (
                BORDER_BACK_EVERY * g,
                BACK_GAP,
                back(
                    [lambda t=t: x_scr[step - 1, t, pl.ds(0, 32), :] for t in ts],
                    lambda g=g: att_scr[g],
                    [store_block(t) for t in ts],
                    w,
                    wup_scr,
                    32 * ts[0],
                    mid_scr,
                    sec_scr,
                    wide_scr,
                    nq=32,
                ),
            )
            for g, ts in enumerate(groups)
        ]

    @pl.when(step == 0)
    def _():
        drive(fronts())

    @pl.when((step > 0) & (step < 4))
    def _():
        drive(backs() + fronts())

    @pl.when(step == 4)
    def _():
        drive(backs())

    def spread(scr, at, first, value):
        for half in range(2):
            scr[2 * at + half, pl.ds(first, count, stride=4), :] = value[:, C * half : C * (half + 1)]

    def both(scr, at, rows):
        return jnp.concatenate([scr[2 * at + half, rows, :] for half in range(2)], axis=1)

    def merged(spots):
        joined = [
            jnp.concatenate([blk_scr[pl.ds(four[n], count, stride=32), :] for four in spots], axis=0)
            for n in range(4)
        ]
        normed = layer_norm(jnp.concatenate(joined, axis=1), w["gm"][...]).astype(BF16)
        out = jnp.dot(normed, w["w_merge"][...], preferred_element_type=F32)
        return [out[count * n : count * (n + 1)] for n in range(len(spots))]

    def row_merged():
        for a in range(2):
            fours = [[(2 * a + dy) * WIN + 2 * b + dx for dx in range(2) for dy in range(2)] for b in range(4)]
            for b, value in enumerate(merged(fours)):
                yield a, b, value

    def col_merged():
        for b in range(2):
            fours = [[(2 * a + dy) * 4 + 2 * b + dx for dx in range(2) for dy in range(2)] for a in range(4)]
            for a, value in enumerate(merged(fours)):
                yield a, b, value

    @pl.when(step == 1)
    def _():
        for a, b, value in row_merged():
            spread(row_scr, a, 8 + b - 2, value)

    @pl.when(step == 2)
    def _():
        for a, b, value in col_merged():
            spread(col_scr, 2 + b, 8 + a - 2, value)

    @pl.when(step == 3)
    def _():
        for a, b, value in row_merged():
            spread(row_scr, 2 + a, 8 + b + 2, value)

    @pl.when(step == 4)
    def _():
        for a, b, value in col_merged():
            spread(col_scr, b, 8 + a + 2, value)

    @pl.when(step == 4)
    def _():
        for c in range(2):
            for a in range(2):
                for h in range(2):
                    row_scr[2 * a + h, pl.ds(8 + OUT - 2 + c, 1), :] = col_scr[2 * (2 + c) + h, pl.ds(8 + a, 1), :]
                    row_scr[2 * (2 + a) + h, pl.ds(8 + c, 1), :] = col_scr[2 * c + h, pl.ds(8 + OUT - 2 + a, 1), :]
        for a in range(4):
            row_out[a] = both(row_scr, a, pl.ds(8, OUT)).astype(BF16)
        for copy in col_in:
            copy.wait()
        place = lax.broadcasted_iota(jnp.int32, (16, 2 * C), 0)
        for side, first in ((0, 0), (1, 14)):
            for r in range(2, OUT - 2):
                old = col_out[side, r].astype(F32)
                for c in range(2):
                    old = jnp.where(place == first + c, both(col_scr, 2 * side + c, pl.ds(8 + r, 1)), old)
                col_out[side, r] = old.astype(BF16)
        inside = pl.ds(2, OUT - 4)
        copies = [
            pltpu.make_async_copy(
                col_out.at[n, inside], out_ref.at[inside, pl.ds(at, 16), :], sem_out.at[n]
            )
            for n, at in enumerate((0, OUT - 16))
        ]
        copies += [
            pltpu.make_async_copy(row_out.at[pl.ds(2 * n, 2)], out_ref.at[pl.ds(at, 2)], sem_out.at[2 + n])
            for n, at in enumerate((0, OUT - 2))
        ]
        for copy in copies:
            copy.start()
        for copy in copies:
            copy.wait()


def border(tokens, ids, got, rel_index, bias_table, weights, inner):
    return pl.pallas_call(
        border_kernel,
        grid=(5,),
        out_shape=jax.ShapeDtypeStruct((OUT, OUT, 2 * C), BF16),
        in_specs=row_specs()
        + col_specs()
        + [whole((STRIPS, SIDE), pltpu.SMEM)]
        + [pl.BlockSpec(memory_space=pl.ANY) for _ in got]
        + [whole(rel_index.shape), whole(bias_table.shape)]
        + [whole(a.shape) for a in weights]
        + [pl.BlockSpec(memory_space=pl.ANY)],
        out_specs=pl.BlockSpec(memory_space=pl.ANY),
        input_output_aliases={11 + len(weights): 0},
        scratch_shapes=[
            pltpu.VMEM((4 * VARIANTS, SPOTS, HEADS * 32), F32),
            pltpu.VMEM((C, C), BF16),
            pltpu.VMEM((C, MLP), BF16),
            pltpu.VMEM((256, 128), F32),
            pltpu.VMEM((16 // GROUP, C, 32 * GROUP), BF16),
            pltpu.VMEM((16 * SPOTS, C), F32),
            pltpu.VMEM((4, 16, SPOTS, C), F32),
            pltpu.VMEM((2 * LINE + 2 * BAND, C), F32),
            pltpu.VMEM((8 * STRIPS, SIDE), jnp.int32),
            pltpu.SMEM((8 * STRIPS, SIDE), jnp.int32),
            pltpu.SMEM((4, 16), jnp.int32),
            pltpu.VMEM((8, OUT + 16, C), F32),
            pltpu.VMEM((8, OUT + 16, C), F32),
            pltpu.VMEM((4, OUT, 2 * C), BF16),
            pltpu.VMEM((2, OUT, 16, 2 * C), BF16),
            pltpu.SemaphoreType.DMA,
            pltpu.SemaphoreType.DMA((2,)),
            pltpu.SemaphoreType.DMA((4,)),
            *[pltpu.VMEM(a.shape, BF16) for a in got],
            pltpu.SemaphoreType.DMA((4,)),
            pltpu.VMEM((16 * SPOTS, C), BF16),
            pltpu.VMEM((16 * SPOTS, C), BF16),
            pltpu.VMEM((16 * SPOTS, C), BF16),
            pltpu.VMEM((C, 16 * SPOTS), BF16),
            pltpu.VMEM((16 * SPOTS, C), F32),
            pltpu.VMEM((16 * SPOTS, C), BF16),
            pltpu.VMEM((16 * SPOTS, MLP), BF16),
            pltpu.VMEM((128, 128), F32),
        ],
        compiler_params=pltpu.CompilerParams(vmem_limit_bytes=26 * 1024 * 1024),
    )(tokens, tokens, tokens, tokens, ids, *got, rel_index, bias_table, *weights, inner)


def on_device(
    tokens, regions, rel_index, bias_table, norm1_gain, w_qkv, w_proj, norm2_gain, w_up, w_down, merge_gain, w_merge
):
    weights = (
        norm1_gain.reshape(1, C), w_qkv, w_proj, norm2_gain.reshape(1, C), w_up, w_down,
        merge_gain.reshape(1, 4 * C), w_merge,
    )
    bias_table = bias_table.T
    tokens = pltpu.with_memory_space_constraint(tokens, pltpu.HBM)
    regions = pltpu.with_memory_space_constraint(regions, pltpu.HBM)
    ids, top, bottom = pack_rows(tokens, regions)
    above, below = moved(bottom, "row", 1), moved(top, "row", -1)
    inner = interior(tokens, ids, rel_index, bias_table, weights, 0, EARLY)
    inner = pltpu.with_memory_space_constraint(inner, pltpu.HBM)
    to_left, to_right, token = pack_cols(tokens, above, below, ids, inner)
    from_left, from_right = moved(to_right, "col", 1), moved(to_left, "col", -1)
    inner = interior(
        tokens, ids, rel_index, bias_table, weights, EARLY, SIDE // WIN - 1 - EARLY, before=inner, after=token
    )
    return border(
        tokens, ids, (above, below, from_left, from_right), rel_index, bias_table, weights, inner
    )


def solution(mesh):
    return jax.shard_map(
        on_device,
        mesh=mesh,
        in_specs=(P("row", "col", None), P("row", "col")) + (P(),) * 10,
        out_specs=P("row", "col", None),
        check_vma=False,
    )
```
